128 devices in a mesh: face: 2 (over x_hi), rows: 64 (over y, z, x_lo, core).
Axes of the slice: x: 4 (x_hi: 2, x_lo: 2; x = x_hi * 2 + x_lo), y: 4, z: 4, core: 2. Of those that a mesh axis runs over, the one named last changes fastest.
Arguments:
- final_adjoint: float32 [16, 6, 1024, 1024], P(None, 'face', 'rows'), may hold values from -6 to 6
- courant_x: float32 [16, 6, 1024, 1024], P(None, 'face', 'rows'), may hold values from 0.05 to 0.45
- courant_y: float32 [16, 6, 1024, 1024], P(None, 'face', 'rows'), may hold values from 0.05 to 0.45
- ray_tiles: bfloat16 [2, 4096, 16, 512], P('face', 'rows'), may hold values from -1.5 to 1.5
- ray_innov: bfloat16 [2, 4096, 16], P('face', 'rows'), may hold values from -6 to 6
- ray_dest: int32 [2, 4096, 1], P('face', 'rows'), may hold values from 0 to 63; in each aligned block of 64 rows (0 to 63, 64 to 127, ..., all dimensions but the last counted through in order) at most 2 rows name the same one
- ray_cols: int32 [2, 4096, 32], P('face', 'rows'), may hold values from 0 to 49151
Outputs:
- prior_adjoint: float32 [16, 6, 1024, 1024], P(None, 'face', 'rows')
The draws below stay inside these ranges and needn't reach their ends.
Inputs may be any that keep to these rules, and one draw needn't show every extreme that they name: `ray_dest`: each device's 64 ray blocks name one band each, at most 2 blocks for one band; some device sends exactly 2 blocks to some band.
All inputs are finite; a program needn't handle non-finite values.
Results may differ from the reference program's by a relative error of at most 0.0003.
Values may be sent and summed in bfloat16 or wider, within the bound.
A program may use at most 128 MiB of HBM per device.

```python
import math
import jax
import jax.numpy as jnp
import numpy as np

FACES = 6
LEV = 16
RD = 16
RAYS = 16
K = 32
BLK_DEV = 64
BANDS = 64
NC = 1024
CAP = 2
N_FACE = 2


def set_ends(values, rng, smallest, largest):
    longest = values.shape.index(max(values.shape))
    spots = []
    for shift in (0, 1):
        where = [jax.random.randint(jax.random.fold_in(rng, axis), (), 0, length) for axis, length in enumerate(values.shape)]
        where[longest] = (where[longest] + shift) % values.shape[longest]
        spots.append(tuple(where))
    return values.at[spots[0]].set(smallest).at[spots[1]].set(largest)


def shard_levels(stream_key, shape, pieces, least, largest):
    level = 1.0
    for axis_at, blocks in pieces:
        steps = jax.random.uniform(jax.random.fold_in(jax.random.fold_in(stream_key, 6), axis_at), (blocks,), jnp.float32, least / len(pieces), largest / len(pieces))
        level = level * jnp.repeat(jnp.exp(steps), shape[axis_at] // blocks).reshape((-1,) + (1,) * (len(shape) - 1 - axis_at))
    return level


def shared_out(key, own, number, rows, number_of, top, most, lean):
    order = jax.random.permutation(key, number_of)
    packed, common = load_shares(number_of, rows * top, most, lean, True), load_shares(number_of, rows * top, most, lean, False)
    places = jnp.arange(number_of)

    def named(tallies, turn):
        used = int((tallies > 0).sum())
        fixed = max(1, used // 4)
        shifted = fixed + (places - fixed + turn * (used - fixed)) % max(1, number_of - fixed)
        return jnp.zeros((number_of,), jnp.int32).at[order[jnp.where(places < fixed, places, shifted)]].set(jnp.asarray(tallies, jnp.int32))

    tallies = jnp.where(number % 4 == 0, named(packed, number // 4), named(common, number - number // 4 - 1))
    mixed = jax.random.permutation(jax.random.fold_in(own, 3), number_of)
    source_of, taker = mixed[0:number_of // 2 * 2:2], mixed[1:number_of // 2 * 2:2]
    slack = jnp.minimum(tallies[source_of] - 1, most - tallies[taker]) // 2
    slack = jnp.where((source_of == order[0]) | (taker == order[0]) | (tallies[taker] == 0), 0, jnp.maximum(slack, 0))
    shifted = jax.random.randint(jax.random.fold_in(own, 4), (number_of // 2,), 0, 1 << 20) % (slack + 1)
    tallies = tallies.at[source_of].add(-shifted).at[taker].add(shifted)
    members = jnp.searchsorted(jnp.cumsum(tallies), jnp.arange(rows * top), side="right").astype(jnp.int32)
    table = members.reshape(top, rows).T
    table = table[jax.random.permutation(jax.random.fold_in(own, 1), rows)]
    turn = jax.random.randint(jax.random.fold_in(own, 2), (rows, 1), 0, top)
    return jnp.take_along_axis(table, (jnp.arange(top)[None, :] + turn) % top, axis=1)


def load_shares(count, total, limit, slope, full):
    loads = [(1 << 20) // math.isqrt(standing ** slope) + 1 for standing in range(1, count + 1)]
    largest = limit if full else min(limit, max(-(-total // count), total * loads[0] // sum(loads)))
    least = 1 if total - largest >= count - 1 else 0
    holding, surplus = [largest] + [least] * (count - 1), total - largest - least * (count - 1)
    while surplus > 0:
        free = [i for i in range(1, count) if holding[i] < largest] or [i for i in range(1, count) if holding[i] < limit]
        pool, left = sum([loads[i] for i in free]), surplus
        for i in free:
            addition = min(limit - holding[i], max(1, left * loads[i] // pool), surplus)
            holding[i] = holding[i] + addition
            surplus = surplus - addition
    return np.array(holding)


def normal_values(own_key, shape, width, bound, pieces=(), held_as=jnp.bfloat16):
    array = jax.random.normal(own_key, shape, jnp.float32) * width
    if len(pieces) > 0:
        array = shard_levels(own_key, shape, pieces, -0.22, 0.18) * array
    return jnp.clip(array, min=-bound, max=bound).astype(held_as)


def setup_inputs(seed: int = 0) -> dict:
    splits = jax.random.split(jax.random.key(seed), 8)
    final_adjoint = normal_values(splits[0], (LEV, FACES, NC, NC), 1.0, 6.0, ((1, 2), (2, 64)), jnp.float32)
    courant_x = jnp.clip(0.05 + 0.39999999 * jax.random.uniform(splits[1], (LEV, FACES, NC, NC), jnp.float32) ** shard_levels(splits[1], (LEV, FACES, NC, NC), ((1, 2), (2, 64)), -0.2, 0.2), 0.05, 0.45)
    courant_y = jnp.clip(0.05 + 0.39999999 * jax.random.uniform(splits[2], (LEV, FACES, NC, NC), jnp.float32) ** shard_levels(splits[2], (LEV, FACES, NC, NC), ((1, 2), (2, 64)), -0.2, 0.2), 0.05, 0.45)
    ray_tiles = normal_values(splits[3], (N_FACE, BANDS * BLK_DEV, RAYS, LEV * K), RAYS ** -0.5, 1.5, ((0, 2), (1, 64)))
    ray_innov = normal_values(splits[4], (N_FACE, BANDS * BLK_DEV, RAYS), 1.0, 6.0, ((0, 2), (1, 64)))
    ray_dest_keys = jax.random.split(jax.random.fold_in(splits[5], 1), N_FACE * (BANDS * BLK_DEV) // BLK_DEV)
    ray_dest_turns = jax.random.permutation(jax.random.fold_in(splits[5], 3), N_FACE * (BANDS * BLK_DEV) // BLK_DEV)
    ray_dest = jax.vmap(lambda own, number: shared_out(jax.random.fold_in(splits[5], 2), own, number, BLK_DEV, BANDS, 1, CAP, 2))(ray_dest_keys, ray_dest_turns).reshape((N_FACE, BANDS * BLK_DEV, 1))
    ray_cols = set_ends(jax.random.randint(splits[6], (N_FACE, BANDS * BLK_DEV, K), 0, 3 * RD * NC), jax.random.fold_in(splits[6], 1), 0, (3 * RD * NC) - 1).astype(jnp.int32)
    return dict(final_adjoint=final_adjoint, courant_x=courant_x, courant_y=courant_y, ray_tiles=ray_tiles, ray_innov=ray_innov, ray_dest=ray_dest, ray_cols=ray_cols)


def forward(field, courant_x, courant_y):
    left_ghost = jnp.roll(field[..., -1], 1, axis=1)
    rotated = field[:, :, ::-1, 0]
    straight = field[:, :, -1, :]
    ghosts = []
    for face_no in range(FACES):
        if face_no % 2 == 0:
            ghosts.append(rotated[:, (face_no + 2) % FACES])
        else:
            ghosts.append(straight[:, (face_no + 1) % FACES])
    top_ghost = jnp.stack(ghosts, axis=1)
    west = jnp.concatenate([left_ghost[..., None], field[..., :-1]], axis=-1)
    north = jnp.concatenate([top_ghost[:, :, None, :], field[:, :, :-1, :]], axis=2)
    return (1.0 - courant_x - courant_y) * field + courant_x * west + courant_y * north

def transpose_step(adjoint, courant_x, courant_y):
    zeros = jnp.zeros_like(adjoint)
    _, pullback = jax.vjp(lambda v: forward(v, courant_x, courant_y), zeros)
    return pullback(adjoint)[0]

def reference(final_adjoint, courant_x, courant_y, ray_tiles, ray_innov, ray_dest, ray_cols):
    contrib = jnp.einsum('gnr,gnrk->gnk', ray_innov.astype(jnp.float32), ray_tiles.astype(jnp.float32))
    groups, blocks = (contrib.shape[0], contrib.shape[1])
    contrib = contrib.reshape(groups, blocks, LEV, K)
    per_group = FACES // N_FACE
    group_id = jnp.arange(groups, dtype=jnp.int32)[:, None, None]
    face_id = per_group * group_id + ray_cols // (RD * NC)
    row_id = ray_dest[..., 0:1] * RD + ray_cols // NC % RD
    col_id = ray_cols % NC
    flat_id = (face_id * NC * NC + row_id * NC + col_id).astype(jnp.int32)
    values = jnp.transpose(contrib, (2, 0, 1, 3)).reshape(LEV, -1)
    forcing = jnp.zeros((LEV, FACES * NC * NC), jnp.float32).at[:, flat_id.reshape(-1)].add(values)
    forcing = forcing.reshape(LEV, FACES, NC, NC)
    mid_adjoint = transpose_step(final_adjoint, courant_x, courant_y) + forcing
    return transpose_step(mid_adjoint, courant_x, courant_y)
```

```python
import functools

import jax
import jax.numpy as jnp
from jax import lax
from jax.experimental import pallas as pl
from jax.experimental.pallas import tpu as pltpu
from jax.sharding import PartitionSpec as P

LEV, LF, RD, NC = 16, 3, 16, 1024
BANDS, RAYS, K, CAP = 64, 16, 32, 2
GROUP = 8
RELAYS = BANDS // GROUP
LANES = 128
PACK = 16
SENT = 9
COPIES = 4
F32, BF16, I32 = jnp.float32, jnp.bfloat16, jnp.int32
MESH = pl.DeviceIdType.MESH


def iota(shape, dim):
    return lax.broadcasted_iota(I32, shape, dim)


def dot(a, b):
    return jnp.dot(a, b, preferred_element_type=F32)


class Halo:
    def __init__(self, tops, sides, below, side_in, rot, sems):
        self.tops, self.sides, self.below, self.side_in, self.rot = tops, sides, below, side_in, rot
        self.send, self.recv, self.rot_send, self.fwd_send, self.rot_recv = sems
        self.g = lax.axis_index("face")
        self.b = lax.axis_index("rows")

    def greet(self, barrier):
        g, b = self.g, self.b

        def hello(face, band):
            pl.semaphore_signal(barrier, inc=1, device_id=(face, band), device_id_type=MESH)

        hello(1 - g, b)

        @pl.when(b < BANDS - 1)
        def _():
            hello(g, b + 1)

        @pl.when(b == BANDS - 1)
        def _():
            hello(g, 0)

        @pl.when((b == BANDS - 1) & (g == 0))
        def _():
            hello(1, 0)

        @pl.when(b % GROUP != 0)
        def _():
            hello(g, b // GROUP * GROUP)

        @pl.when(b % GROUP == 0)
        def _():
            hello(1 - g, 0)

        @pl.when((b % GROUP == 0) & (g == 0) & (b != 0))
        def _():
            hello(0, 0)

        relay = (b % GROUP == 0).astype(I32)
        origin = (b == 0).astype(I32)
        return 2 + relay * (GROUP - 1) + origin * (RELAYS + jnp.where(g == 0, RELAYS - 1, 1))

    def zero(self):
        g, b = self.g, self.b
        edge = jnp.zeros((LEV, NC), F32)

        @pl.when(b == BANDS - 1)
        def _():
            @pl.when(g == 0)
            def _():
                self.below[1] = edge

            @pl.when(g == 1)
            def _():
                self.below[0] = edge
                self.below[2] = edge

        @pl.when(g == 1)
        def _():
            self.rot[1] = jnp.zeros((LEV, LANES), F32)

    def copy(self, src, dst, send, recv, face, band):
        return pltpu.make_async_remote_copy(
            src_ref=src, dst_ref=dst, send_sem=send, recv_sem=recv,
            device_id=(face, band), device_id_type=MESH,
        )

    def row(self, face):
        return self.copy(self.tops, self.below, self.send.at[0], self.recv.at[0], self.g, face)

    def one(self, src, dst, face, slot):
        return self.copy(
            self.tops.at[src], self.below.at[dst], self.send.at[slot], self.recv.at[slot], face, BANDS - 1
        )

    def side(self):
        return self.copy(self.sides, self.side_in, self.send.at[1], self.recv.at[1], 1 - self.g, self.b)

    def piece(self, src, dst, face, r, n):
        lanes = pl.ds(LANES * (RELAYS - 1 - r), LANES)
        return self.copy(
            self.tops.at[src, :, lanes], self.rot.at[dst], self.rot_send.at[dst, r], self.rot_recv.at[dst],
            face, n,
        )

    def start(self):
        g, b = self.g, self.b

        @pl.when(b == 0)
        def _():
            @pl.when(g == 0)
            def _():
                for r in range(RELAYS):
                    self.piece(2, 0, 1, r, r * GROUP).start()
                for r in range(1, RELAYS):
                    self.piece(0, 1, 0, r, r * GROUP).start()
                self.one(1, 2, 0, 0).start()
                self.rot[1] = self.tops[0, :, NC - LANES :]

            @pl.when(g == 1)
            def _():
                for r in range(RELAYS):
                    self.piece(1, 0, 0, r, r * GROUP).start()
                self.one(0, 1, 1, 0).start()
                self.one(2, 0, 0, 2).start()

        @pl.when(b != 0)
        def _():
            self.row(b - 1).start()

        self.side().start()

    def forward(self, dst, i):
        return self.copy(
            self.rot.at[dst], self.rot.at[dst], self.fwd_send.at[dst, i], self.rot_recv.at[dst],
            self.g, self.b // GROUP * GROUP + i,
        )

    def relay(self):
        g, b = self.g, self.b

        @pl.when(b % GROUP == 0)
        def _():
            self.forward(0, 1).wait_recv()
            for i in range(1, GROUP):
                self.forward(0, i).start()

            @pl.when(g == 0)
            def _():
                @pl.when(b != 0)
                def _():
                    self.forward(1, 1).wait_recv()

                for i in range(1, GROUP):
                    self.forward(1, i).start()

    def wait(self):
        g, b = self.g, self.b

        @pl.when(b % GROUP != 0)
        def _():
            self.forward(0, 1).wait_recv()

            @pl.when(g == 0)
            def _():
                self.forward(1, 1).wait_recv()

        self.side().wait_recv()

        @pl.when(b != BANDS - 1)
        def _():
            self.row(0).wait_recv()

        @pl.when(b == BANDS - 1)
        def _():
            @pl.when(g == 0)
            def _():
                self.one(1, 2, 0, 0).wait_recv()
                self.one(2, 0, 0, 2).wait_recv()

            @pl.when(g == 1)
            def _():
                self.one(0, 1, 1, 0).wait_recv()

    def finish(self):
        g, b = self.g, self.b
        self.side().wait_send()

        @pl.when(b != 0)
        def _():
            self.row(0).wait_send()

        @pl.when(b == 0)
        def _():
            @pl.when(g == 0)
            def _():
                for r in range(RELAYS):
                    self.piece(2, 0, 1, r, r * GROUP).wait_send()
                for r in range(1, RELAYS):
                    self.piece(0, 1, 0, r, r * GROUP).wait_send()
                self.one(1, 2, 0, 0).wait_send()

            @pl.when(g == 1)
            def _():
                for r in range(RELAYS):
                    self.piece(1, 0, 0, r, r * GROUP).wait_send()
                self.one(0, 1, 1, 0).wait_send()
                self.one(2, 0, 0, 2).wait_send()

        @pl.when(b % GROUP == 0)
        def _():
            for i in range(1, GROUP):
                self.forward(0, i).wait_send()

            @pl.when(g == 0)
            def _():
                for i in range(1, GROUP):
                    self.forward(1, i).wait_send()


def halo_scratch():
    return [
        pltpu.VMEM((LF, LEV, NC), F32),
        pltpu.VMEM((RD, LANES), F32),
        pltpu.VMEM((LF, LEV, NC), F32),
        pltpu.VMEM((RD, LANES), F32),
        pltpu.VMEM((2, LEV, LANES), F32),
        pltpu.SemaphoreType.DMA((3,)),
        pltpu.SemaphoreType.DMA((3,)),
        pltpu.SemaphoreType.DMA((2, RELAYS)),
        pltpu.SemaphoreType.DMA((2, GROUP)),
        pltpu.SemaphoreType.DMA((2,)),
    ]


def edges(a, cx, cy, tops, sides):
    lane = iota((RD, LANES), 1)

    def body(l, acc):
        for f in range(LF):
            tops[f, pl.ds(l, 1), :] = cy[l, f, 0:1, :] * a[l, f, 0:1, :]
        along = cx[l, 0, :, 0:LANES] * a[l, 0, :, 0:LANES]
        return jnp.where(lane == l, jnp.broadcast_to(along[:, 0:1], (RD, LANES)), acc)

    sides[...] = lax.fori_loop(0, LEV, body, jnp.zeros((RD, LANES), F32))


def interior(a, cx, cy, out, lo, hi):
    row = iota((RD, NC), 0)
    col = iota((RD, NC), 1)

    def body(l, carry):
        base, rolled = [], []
        for f in range(LF):
            value, x, y = a[l, f], cx[l, f], cy[l, f]
            along, upward = x * value, y * value
            rolled.append(pltpu.roll(along, NC - 1, 1))
            lifted = jnp.where(row < RD - 1, pltpu.roll(upward, RD - 1, 0), 0.0)
            base.append((1.0 - x - y) * value + lifted)
        for f in range(LF):
            beyond = rolled[f + 1] if f + 1 < LF else 0.0
            out[l, f] = base[f] + jnp.where(col < NC - 1, rolled[f], beyond)
        return carry

    lax.fori_loop(lo, hi, body, 0)


def patch(out, below, side_in, rot):
    g = lax.axis_index("face")
    b = lax.axis_index("rows")
    row = iota((8, NC), 0)
    lane = iota((RD, LANES), 1)
    place = LANES - 1 - RD * (b % GROUP) - iota((RD, LANES), 0)

    def body(l, carry):
        for f in range(LF):
            edge = jnp.broadcast_to(below[f, pl.ds(l, 1), :], (8, NC))
            out[l, f, 8:RD, :] += jnp.where(row == 7, edge, 0.0)

        def column(piece):
            picked = jnp.where(lane == place, jnp.broadcast_to(piece, (RD, LANES)), 0.0)
            return jnp.where(lane == 0, jnp.sum(picked, axis=1, keepdims=True), 0.0)

        cross = column(rot[0, pl.ds(l, 1), :])
        local = column(rot[1, pl.ds(l, 1), :])
        right = jnp.sum(jnp.where(lane == l, side_in[...], 0.0), axis=1, keepdims=True)
        out[l, 0, :, 0:LANES] += jnp.where(g == 0, cross, 0.0)
        out[l, 1, :, 0:LANES] += jnp.where(g == 1, cross, 0.0)
        out[l, 2, :, 0:LANES] += local
        out[l, 2, :, NC - LANES :] += jnp.where(lane == LANES - 1, right, 0.0)
        return carry

    lax.fori_loop(0, LEV, body, 0)


def pack(tiles, innov, dest, cells, send):
    blocks = BANDS
    wide = blocks * RAYS
    spread = (iota((RAYS, wide), 1) % RAYS == iota((RAYS, wide), 0)).astype(BF16)
    own = iota((blocks, wide), 1) // RAYS == iota((blocks, wide), 0)
    diag = jnp.where(own, dot(innov[0], spread), 0.0).astype(BF16)

    target = jnp.broadcast_to(dest[0], (blocks, blocks))
    before, after = iota((blocks, blocks), 0), iota((blocks, blocks), 1)
    targets = jnp.sum(jnp.where(before == after, target, 0).astype(F32), axis=0, keepdims=True)
    same = (target.astype(F32) == targets) & (before < after)
    orders = jnp.sum(same.astype(F32), axis=0, keepdims=True)
    slot = iota((CAP * BANDS, blocks), 0)
    chosen = ((slot % BANDS).astype(F32) == targets) & ((slot // BANDS).astype(F32) == orders)
    chosen = chosen.astype(BF16)

    src, dst = iota((LEV * K, LEV * K), 0), iota((LEV * K, LEV * K), 1)
    level, part, inner = dst % LANES // 8, dst // LANES, dst % 8
    mixed = (src == level * K + part * 8 + inner).astype(BF16)
    weights = dot(tiles[0].reshape(wide, LEV * K), mixed).astype(BF16)
    sums = dot(dot(chosen, diag).astype(BF16), weights)

    cell = cells[0]
    code = ((cell // (8 * NC)) * NC + cell % NC) * 8 + cell // NC % 8
    high, low = (code // 256).astype(F32).astype(BF16), (code % 256).astype(F32).astype(BF16)
    codes = dot(chosen, high) * 256.0 + dot(chosen, low)
    codes = jnp.concatenate(
        [codes[:BANDS], codes[BANDS:], jnp.zeros((BANDS, LANES - 2 * K), F32)], axis=1
    )
    flat = send.reshape(BANDS * PACK, LANES)
    for s in range(CAP):
        for q in range(4):
            flat[pl.ds(s * 4 + q, BANDS, stride=PACK), :] = sums[
                s * BANDS : (s + 1) * BANDS, q * LANES : (q + 1) * LANES
            ]
    flat[pl.ds(SENT - 1, BANDS, stride=PACK), :] = codes


def first_kernel(
    a_hbm, cx_hbm, cy_hbm, tiles, innov, dest, cells, out, recv,
    a, cx, cy, send, load_sem, pack_send, pack_recv, own_sem, tops, sides, below, side_in, rot, *sems,
):
    g = lax.axis_index("face")
    b = lax.axis_index("rows")
    loads = [
        pltpu.make_async_copy(src, dst, load_sem.at[i])
        for i, (src, dst) in enumerate(((a_hbm, a), (cy_hbm, cy), (cx_hbm, cx)))
    ]
    for load in loads:
        load.start()
    halo = Halo(tops, sides, below, side_in, rot, sems)
    barrier = pltpu.get_barrier_semaphore()
    expected = halo.greet(barrier) + BANDS - 1

    def hello(i, carry):
        pl.semaphore_signal(barrier, inc=1, device_id=(g, (b + i) % BANDS), device_id_type=MESH)
        return carry

    lax.fori_loop(1, BANDS, hello, 0)
    halo.zero()
    pack(tiles, innov, dest, cells, send)
    pl.semaphore_wait(barrier, expected)

    def packet(band):
        return pltpu.make_async_remote_copy(
            src_ref=send.at[band, pl.ds(0, SENT)],
            dst_ref=recv.at[b, pl.ds(0, SENT)],
            send_sem=pack_send,
            recv_sem=pack_recv.at[b],
            device_id=(g, band),
            device_id_type=MESH,
        )

    def ship(i, carry):
        packet((b + i) % BANDS).start()
        return carry

    lax.fori_loop(1, BANDS, ship, 0)
    own = pltpu.make_async_copy(send.at[b, pl.ds(0, SENT)], recv.at[b, pl.ds(0, SENT)], own_sem)
    own.start()
    for load in loads:
        load.wait()
    edges(a, cx, cy, tops, sides)
    halo.start()
    interior(a, cx, cy, out, 0, LEV // 2)
    halo.relay()
    interior(a, cx, cy, out, LEV // 2, LEV)
    halo.wait()
    patch(out, below, side_in, rot)
    halo.finish()
    own.wait()

    def landed(i, carry):
        band = (b + i) % BANDS
        pltpu.make_async_remote_copy(
            src_ref=send.at[band, pl.ds(0, SENT)],
            dst_ref=recv.at[band, pl.ds(0, SENT)],
            send_sem=pack_send,
            recv_sem=pack_recv.at[band],
            device_id=(g, band),
            device_id_type=MESH,
        ).wait()
        return carry

    lax.fori_loop(1, BANDS, landed, 0)


def scatter_kernel(recv, dense_hbm, out, dense, index, index_s, values, *rest):
    fields, (load_sem, index_sem) = rest[:COPIES], rest[COPIES:]
    load = pltpu.make_async_copy(dense_hbm, dense, load_sem)
    load.start()
    flat = recv.reshape(BANDS * PACK, LANES)
    index[...] = flat[pl.ds(SENT - 1, BANDS, stride=PACK), :].astype(I32)
    to_scalar = pltpu.make_async_copy(index, index_s, index_sem)
    to_scalar.start()

    step = 8
    rows = step * CAP * 4
    inner = iota((rows, 8, LANES), 2) % 8 == iota((rows, 8, LANES), 1)
    widen = (iota((LANES, LANES), 0) // 8 == iota((LANES, LANES), 1) // 8).astype(BF16)

    def expand(i, carry):
        got = recv[pl.ds(i * step, step), 0 : CAP * 4, :].reshape(rows, 1, LANES)
        one = jnp.where(inner, jnp.broadcast_to(got, (rows, 8, LANES)), 0.0).reshape(rows * 8, LANES)
        high = one.astype(BF16)
        rest = one - high.astype(F32)
        mid = rest.astype(BF16)
        low = (rest - mid.astype(F32)).astype(BF16)
        values[pl.ds(i * rows * 8, rows * 8), :] = dot(high, widen) + dot(mid, widen) + dot(low, widen)
        return carry

    lax.fori_loop(0, BANDS // step, expand, 0)

    def clear(i, carry):
        for field in fields:
            field[pl.ds(i * LANES, LANES), :] = jnp.zeros((LANES, LANES), F32)
        return carry

    lax.fori_loop(0, LF * 2 * NC // LANES, clear, 0)
    to_scalar.wait()
    lane = iota((1, LANES), 1) % 8
    entries = CAP * K

    def add(i, carry):
        for e in range(entries):
            code = index_s[i, e]
            line = values[pl.ds(i * entries + e, 1), :]
            field = fields[e % COPIES]
            field[pl.ds(code // 8, 1), :] += jnp.where(lane == code % 8, line, 0.0)
        return carry

    lax.fori_loop(0, BANDS, add, 0)
    load.wait()

    def turn(i, carry):
        f, half = i // 2, i % 2
        for c in range(NC // LANES):
            block = sum(field[pl.ds(i * NC + c * LANES, LANES), :] for field in fields)
            turned = block.T.reshape(LEV, 8, LANES)
            rows = pl.ds(pl.multiple_of(half * 8, 8), 8)
            cols = pl.ds(c * LANES, LANES)
            out[:, f, rows, cols] = dense[:, f, rows, cols] + turned
        return carry

    lax.fori_loop(0, LF * 2, turn, 0)


def last_kernel(
    a_hbm, cx_hbm, cy_hbm, out, a, cx, cy, load_sem, tops, sides, below, side_in, rot, *sems
):
    loads = [
        pltpu.make_async_copy(src, dst, load_sem.at[i])
        for i, (src, dst) in enumerate(((a_hbm, a), (cy_hbm, cy), (cx_hbm, cx)))
    ]
    for load in loads:
        load.start()
    halo = Halo(tops, sides, below, side_in, rot, sems)
    barrier = pltpu.get_barrier_semaphore()
    expected = halo.greet(barrier)
    halo.zero()
    for load in loads:
        load.wait()
    edges(a, cx, cy, tops, sides)
    pl.semaphore_wait(barrier, expected)
    halo.start()
    interior(a, cx, cy, out, 0, LEV // 2)
    halo.relay()
    interior(a, cx, cy, out, LEV // 2, LEV)
    halo.wait()
    patch(out, below, side_in, rot)
    halo.finish()


FIELD = (LEV, LF, RD, NC)


def params(cid=None):
    kw = {} if cid is None else dict(collective_id=cid, has_side_effects=True)
    return pltpu.CompilerParams(vmem_limit_bytes=48 * 1024 * 1024, **kw)


def per_device(final_adjoint, courant_x, courant_y, ray_tiles, ray_innov, ray_dest, ray_cols):
    vmem, anywhere = pl.BlockSpec(memory_space=pltpu.VMEM), pl.BlockSpec(memory_space=pl.ANY)
    field = jax.ShapeDtypeStruct(FIELD, F32)
    held = pltpu.VMEM(FIELD, F32)
    dense, recv = pl.pallas_call(
        first_kernel,
        out_shape=(field, jax.ShapeDtypeStruct((BANDS, PACK, LANES), F32)),
        in_specs=[anywhere] * 3 + [vmem] * 4,
        out_specs=(vmem, anywhere),
        scratch_shapes=[
            held, held, held,
            pltpu.VMEM((BANDS, PACK, LANES), F32),
            pltpu.SemaphoreType.DMA((3,)),
            pltpu.SemaphoreType.DMA,
            pltpu.SemaphoreType.DMA((BANDS,)),
            pltpu.SemaphoreType.DMA,
        ] + halo_scratch(),
        compiler_params=params(0),
        name="sums_and_first_step",
    )(final_adjoint, courant_x, courant_y, ray_tiles, ray_innov, ray_dest, ray_cols)
    mid = pl.pallas_call(
        scatter_kernel,
        out_shape=field,
        in_specs=[vmem, anywhere],
        out_specs=vmem,
        scratch_shapes=[
            held,
            pltpu.VMEM((BANDS, LANES), I32),
            pltpu.SMEM((BANDS, LANES), I32),
            pltpu.VMEM((BANDS * CAP * K, LANES), F32),
        ] + [pltpu.VMEM((LF * 2 * NC, LANES), F32)] * COPIES + [
            pltpu.SemaphoreType.DMA,
            pltpu.SemaphoreType.DMA,
        ],
        compiler_params=params(),
        name="forcing",
    )(recv, dense)
    return pl.pallas_call(
        last_kernel,
        out_shape=field,
        in_specs=[anywhere] * 3,
        out_specs=vmem,
        scratch_shapes=[held, held, held, pltpu.SemaphoreType.DMA((3,))] + halo_scratch(),
        compiler_params=params(1),
        name="second_step",
    )(mid, courant_x, courant_y)


def solution(mesh):
    placed = (
        P(None, "face", "rows", None),
        P(None, "face", "rows", None),
        P(None, "face", "rows", None),
        P("face", "rows", None, None),
        P("face", "rows", None),
        P("face", "rows", None),
        P("face", "rows", None),
    )
    return jax.shard_map(
        per_device,
        mesh=mesh,
        in_specs=placed,
        out_specs=P(None, "face", "rows", None),
        check_vma=False,
    )
```

```python
import functools

import jax
import jax.numpy as jnp
from jax import lax
from jax.experimental import pallas as pl
from jax.experimental.pallas import tpu as pltpu
from jax.sharding import PartitionSpec as P

LEV, LF, RD, NC = 16, 3, 16, 1024
BANDS, RAYS, K, CAP = 64, 16, 32, 2
GROUP = 8
RELAYS = BANDS // GROUP
LANES = 128
PACK = 16
SENT = 9
COPIES = 4
F32, BF16, I32 = jnp.float32, jnp.bfloat16, jnp.int32
MESH = pl.DeviceIdType.MESH


def iota(shape, dim):
    return lax.broadcasted_iota(I32, shape, dim)


def dot(a, b):
    return jnp.dot(a, b, preferred_element_type=F32)


def dot_t(a, b):
    return lax.dot_general(a, b, (((1,), (1,)), ((), ())), preferred_element_type=F32)


def split(value):
    high = value.astype(BF16)
    rest = value - high.astype(F32)
    mid = rest.astype(BF16)
    return high, mid, rest - mid.astype(F32)


class Halo:
    def __init__(self, ups, sides, below, side_in, rot, sems):
        self.ups, self.sides, self.below, self.side_in, self.rot = ups, sides, below, side_in, rot
        self.send, self.recv, self.rot_send, self.fwd_send, self.rot_recv = sems
        self.g = lax.axis_index("face")
        self.b = lax.axis_index("rows")

    def greet(self, barrier):
        g, b = self.g, self.b

        def hello(face, band):
            pl.semaphore_signal(barrier, inc=1, device_id=(face, band), device_id_type=MESH)

        hello(1 - g, b)

        @pl.when(b < BANDS - 1)
        def _():
            hello(g, b + 1)

        @pl.when(b == BANDS - 1)
        def _():
            hello(g, 0)

        @pl.when((b == BANDS - 1) & (g == 0))
        def _():
            hello(1, 0)

        @pl.when((b & (GROUP - 1)) != 0)
        def _():
            hello(g, b & -GROUP)

        @pl.when((b & (GROUP - 1)) == 0)
        def _():
            hello(1 - g, 0)

        @pl.when(((b & (GROUP - 1)) == 0) & (g == 0) & (b != 0))
        def _():
            hello(0, 0)

        relay = ((b & (GROUP - 1)) == 0).astype(I32)
        origin = (b == 0).astype(I32)
        return 2 + relay * (GROUP - 1) + origin * (RELAYS + jnp.where(g == 0, RELAYS - 1, 1))

    def zero(self):
        g, b = self.g, self.b
        edge = jnp.zeros((LEV, 1, NC), F32)

        @pl.when(b == BANDS - 1)
        def _():
            @pl.when(g == 0)
            def _():
                self.below[:, 1] = edge

            @pl.when(g == 1)
            def _():
                self.below[:, 0] = edge
                self.below[:, 2] = edge

        @pl.when(g == 1)
        def _():
            self.rot[1] = jnp.zeros((LEV, 1, LANES), F32)

    def copy(self, src, dst, send, recv, face, band):
        return pltpu.make_async_remote_copy(
            src_ref=src, dst_ref=dst, send_sem=send, recv_sem=recv,
            device_id=(face, band), device_id_type=MESH,
        )

    def row(self, face):
        return self.copy(self.ups.at[:, :, 0:1, :], self.below, self.send.at[0], self.recv.at[0], self.g, face)

    def one(self, src, dst, face, slot):
        return self.copy(
            self.ups.at[:, src, 0:1, :], self.below.at[:, dst], self.send.at[slot], self.recv.at[slot], face, BANDS - 1
        )

    def side(self):
        return self.copy(self.sides, self.side_in, self.send.at[1], self.recv.at[1], 1 - self.g, self.b)

    def piece(self, src, dst, face, r, n):
        lanes = pl.ds(LANES * (RELAYS - 1 - r), LANES)
        return self.copy(
            self.ups.at[:, src, 0:1, lanes], self.rot.at[dst], self.rot_send.at[dst, r], self.rot_recv.at[dst],
            face, n,
        )

    def start(self):
        g, b = self.g, self.b

        @pl.when(b == 0)
        def _():
            @pl.when(g == 0)
            def _():
                for r in range(RELAYS):
                    self.piece(2, 0, 1, r, r * GROUP).start()
                for r in range(1, RELAYS):
                    self.piece(0, 1, 0, r, r * GROUP).start()
                self.one(1, 2, 0, 0).start()
                self.rot[1] = self.ups[:, 0, 0:1, NC - LANES :]

            @pl.when(g == 1)
            def _():
                for r in range(RELAYS):
                    self.piece(1, 0, 0, r, r * GROUP).start()
                self.one(0, 1, 1, 0).start()
                self.one(2, 0, 0, 2).start()

        @pl.when(b != 0)
        def _():
            self.row(b - 1).start()

        self.side().start()

    def forward(self, dst, i):
        return self.copy(
            self.rot.at[dst], self.rot.at[dst], self.fwd_send.at[dst, i], self.rot_recv.at[dst],
            self.g, (self.b & -GROUP) + i,
        )

    def relay(self):
        g, b = self.g, self.b

        @pl.when((b & (GROUP - 1)) == 0)
        def _():
            self.forward(0, 1).wait_recv()
            for i in range(1, GROUP):
                self.forward(0, i).start()

            @pl.when(g == 0)
            def _():
                @pl.when(b != 0)
                def _():
                    self.forward(1, 1).wait_recv()

                for i in range(1, GROUP):
                    self.forward(1, i).start()

    def wait_rotated(self):
        g, b = self.g, self.b

        @pl.when((b & (GROUP - 1)) != 0)
        def _():
            self.forward(0, 1).wait_recv()

            @pl.when(g == 0)
            def _():
                self.forward(1, 1).wait_recv()

    def wait_rows(self):
        g, b = self.g, self.b
        self.side().wait_recv()

        @pl.when(b != BANDS - 1)
        def _():
            self.row(0).wait_recv()

        @pl.when(b == BANDS - 1)
        def _():
            @pl.when(g == 0)
            def _():
                self.one(1, 2, 0, 0).wait_recv()
                self.one(2, 0, 0, 2).wait_recv()

            @pl.when(g == 1)
            def _():
                self.one(0, 1, 1, 0).wait_recv()

    def finish(self):
        g, b = self.g, self.b
        self.side().wait_send()

        @pl.when(b != 0)
        def _():
            self.row(0).wait_send()

        @pl.when(b == 0)
        def _():
            @pl.when(g == 0)
            def _():
                for r in range(RELAYS):
                    self.piece(2, 0, 1, r, r * GROUP).wait_send()
                for r in range(1, RELAYS):
                    self.piece(0, 1, 0, r, r * GROUP).wait_send()
                self.one(1, 2, 0, 0).wait_send()

            @pl.when(g == 1)
            def _():
                for r in range(RELAYS):
                    self.piece(1, 0, 0, r, r * GROUP).wait_send()
                self.one(0, 1, 1, 0).wait_send()
                self.one(2, 0, 0, 2).wait_send()

        @pl.when((b & (GROUP - 1)) == 0)
        def _():
            for i in range(1, GROUP):
                self.forward(0, i).wait_send()

            @pl.when(g == 0)
            def _():
                for i in range(1, GROUP):
                    self.forward(1, i).wait_send()


def halo_in():
    return [
        pltpu.VMEM((LEV, LF, 1, NC), F32),
        pltpu.VMEM((RD, LANES), F32),
        pltpu.VMEM((2, LEV, 1, LANES), F32),
        pltpu.SemaphoreType.DMA((3,)),
        pltpu.SemaphoreType.DMA((3,)),
        pltpu.SemaphoreType.DMA((2, RELAYS)),
        pltpu.SemaphoreType.DMA((2, GROUP)),
        pltpu.SemaphoreType.DMA((2,)),
    ]


UPS = (LEV, LF, 8, NC)
SIDES = (RD, LANES)
FIELD = (LEV, LF, RD, NC)


def west(a, cx, sides):
    along = cx[:, 0, :, 0:LANES] * a[:, 0, :, 0:LANES]
    lane = iota(SIDES, 1)
    total = jnp.zeros(SIDES, F32)
    for l in range(LEV):
        total = jnp.where(lane == l, jnp.broadcast_to(along[l, :, 0:1], SIDES), total)
    sides[...] = total


def interior(a, cx, cy, out, lo, hi):
    row = iota((RD, NC), 0)
    col = iota((RD, NC), 1)

    def body(l, carry):
        base, rolled = [], []
        for f in range(LF):
            value, x, y = a[l, f], cx[l, f], cy[l, f]
            along, upward = x * value, y * value
            rolled.append(pltpu.roll(along, NC - 1, 1))
            lifted = jnp.where(row < RD - 1, pltpu.roll(upward, RD - 1, 0), 0.0)
            base.append((1.0 - x - y) * value + lifted)
        for f in range(LF):
            beyond = rolled[f + 1] if f + 1 < LF else 0.0
            out[l, f] = base[f] + jnp.where(col < NC - 1, rolled[f], beyond)
        return carry

    lax.fori_loop(lo, hi, body, 0)


def patch_rows(out, below, side_in):
    def body(l, carry):
        for f in range(LF):
            out[l, f, RD - 1 : RD, :] += below[l, f]
        return carry

    lax.fori_loop(0, LEV, body, 0)
    full = (LEV, RD, LANES)
    lane = iota(full, 2)
    mine = jnp.where(lane == iota(full, 0), jnp.broadcast_to(side_in[...][None], full), 0.0)
    right = jnp.sum(mine, axis=2, keepdims=True)
    out[:, 2, :, NC - LANES :] += jnp.where(lane == LANES - 1, right, 0.0)


def patch_rotated(out, rot):
    g = lax.axis_index("face")
    b = lax.axis_index("rows")
    full = (LEV, RD, LANES)
    lane = iota(full, 2)
    place = LANES - 1 - RD * (b & (GROUP - 1)) - iota(full, 1)

    def column(piece):
        picked = jnp.where(lane == place, jnp.broadcast_to(piece, full), 0.0)
        return jnp.where(lane == 0, jnp.sum(picked, axis=2, keepdims=True), 0.0)

    out[:, pl.ds(g, 1), :, 0:LANES] += column(rot[0]).reshape(LEV, 1, RD, LANES)

    @pl.when(g == 0)
    def _():
        out[:, 2, :, 0:LANES] += column(rot[1])


def pack(tiles, innov, dest, cells, send):
    blocks = BANDS
    wide = blocks * RAYS
    ray = iota((RAYS, wide), 1) & (RAYS - 1)
    repeat = (lax.shift_right_logical(iota((blocks, wide), 1), 4) == iota((blocks, wide), 0)).astype(BF16)
    lines = jnp.where(ray == iota((RAYS, wide), 0), dot(innov[0], repeat), 0.0)
    weight = jnp.sum(lines, axis=0, keepdims=True)

    square = (blocks, blocks)
    first, second = iota(square, 0), iota(square, 1)
    target = jnp.broadcast_to(dest[0].astype(F32), square)
    other = dot(jnp.where(first == second, target, 0.0).astype(BF16), jnp.ones(square, BF16))
    same = (other == target) & (first < second)
    order = jnp.sum(same.astype(F32), axis=0, keepdims=True)
    slot = iota((CAP * BANDS, blocks), 0)
    band = ((slot + lax.axis_index("rows")) & (BANDS - 1)).astype(F32)
    turn = lax.shift_right_logical(slot, 6).astype(F32)
    chosen = ((band == target[0:1]) & (turn == order)).astype(BF16)

    sums = dot((dot(chosen, repeat) * weight).astype(BF16), tiles[0].reshape(wide, LEV * K))
    src, dst = iota((LEV * K, LEV * K), 0), iota((LEV * K, LEV * K), 1)
    level = lax.shift_right_logical(dst & (LANES - 1), 3)
    part = lax.shift_right_logical(dst, 7)
    mixed = (src == level * K + part * 8 + (dst & 7)).astype(BF16)
    high, mid, low = split(sums)
    sums = dot(high, mixed) + dot(mid, mixed) + dot(low.astype(BF16), mixed)

    cell = cells[0]
    shift = lax.shift_right_logical
    code = ((shift(cell, 13) * NC + (cell & (NC - 1))) * 8) + (shift(cell, 10) & 7)
    upper, lower = shift(code, 8).astype(F32).astype(BF16), (code & 255).astype(F32).astype(BF16)
    codes = dot_t(chosen, upper) * 256.0 + dot_t(chosen, lower)
    codes = jnp.concatenate(
        [codes[:BANDS], codes[BANDS:], jnp.zeros((BANDS, LANES - 2 * K), F32)], axis=1
    )
    flat = send.reshape(BANDS * PACK, LANES)
    for s in range(CAP):
        for q in range(4):
            flat[pl.ds(s * 4 + q, BANDS, stride=PACK), :] = sums[
                s * BANDS : (s + 1) * BANDS, q * LANES : (q + 1) * LANES
            ]
    flat[pl.ds(SENT - 1, BANDS, stride=PACK), :] = codes


def first_kernel(
    a_hbm, cx_hbm, cy_hbm, tiles_hbm, innov_hbm, dest_hbm, cells_hbm, out, recv, cx, cy,
    a, tiles, innov, dest, cells, send, load_sem, pack_send, pack_recv, own_sem, ups, sides,
    below, side_in, rot, *sems,
):
    g = lax.axis_index("face")
    b = lax.axis_index("rows")
    pairs = (
        (innov_hbm, innov), (dest_hbm, dest), (cells_hbm, cells), (tiles_hbm, tiles),
        (a_hbm, a), (cy_hbm, cy), (cx_hbm, cx),
    )
    loads = [pltpu.make_async_copy(src, dst, load_sem.at[i]) for i, (src, dst) in enumerate(pairs)]
    for load in loads:
        load.start()
    halo = Halo(ups, sides, below, side_in, rot, sems)
    barrier = pltpu.get_barrier_semaphore()
    expected = halo.greet(barrier) + BANDS - 1

    def hello(i, carry):
        pl.semaphore_signal(barrier, inc=1, device_id=(g, (b + i) & (BANDS - 1)), device_id_type=MESH)
        return carry

    lax.fori_loop(1, BANDS, hello, 0)
    halo.zero()
    for load in loads[:4]:
        load.wait()
    pack(tiles, innov, dest, cells, send)
    own = pltpu.make_async_copy(send.at[0, pl.ds(0, SENT)], recv.at[0, pl.ds(0, SENT)], own_sem)
    own.start()
    for load in loads[4:]:
        load.wait()

    def lift(l, carry):
        ups[l] = cy[l, :, 0:8, :] * a[l, :, 0:8, :]
        return carry

    lax.fori_loop(0, LEV, lift, 0)
    west(a, cx, sides)
    pl.semaphore_wait(barrier, expected)
    halo.start()

    def packets(which, band):
        return pltpu.make_async_remote_copy(
            src_ref=send.at[which, pl.ds(0, SENT)],
            dst_ref=recv.at[which, pl.ds(0, SENT)],
            send_sem=pack_send,
            recv_sem=pack_recv,
            device_id=(g, band),
            device_id_type=MESH,
        )

    def ship(i, carry):
        packets(i, (b + i) & (BANDS - 1)).start()
        return carry

    lax.fori_loop(1, BANDS, ship, 0)
    halo.relay()
    interior(a, cx, cy, out, 0, LEV)
    halo.wait_rows()
    patch_rows(out, below, side_in)
    halo.wait_rotated()
    patch_rotated(out, rot)
    halo.finish()
    own.wait()
    packets(pl.ds(1, BANDS - 1), b).wait()


def scatter_kernel(recv, dense, cx, cy, out, ups, sides, index, index_s, values, *rest):
    fields, (index_sem,) = rest[:COPIES], rest[COPIES:]
    flat = recv.reshape(BANDS * PACK, LANES)
    index[...] = flat[pl.ds(SENT - 1, BANDS, stride=PACK), :].astype(I32)
    to_scalar = pltpu.make_async_copy(index, index_s, index_sem)
    to_scalar.start()

    shift = lax.shift_right_logical
    from_lane, to_lane = iota((2 * LANES, 8 * LANES), 0), iota((2 * LANES, 8 * LANES), 1)
    from_lane = from_lane & (LANES - 1)
    widen = (shift(from_lane, 3) == shift(to_lane & (LANES - 1), 3)) & ((from_lane & 7) == shift(to_lane, 7))
    widen = widen.astype(F32).astype(BF16)
    got = recv[:, 0 : CAP * 4, :].reshape(BANDS * CAP * 4, LANES)
    high, mid, _ = split(got)
    wide = dot(jnp.concatenate([high, mid], axis=1), widen)
    values[...] = wide.reshape(BANDS, CAP * 4, 8 * LANES)

    def clear(i, carry):
        for field in fields:
            field[pl.ds(i * LANES, LANES), :] = jnp.zeros((LANES, LANES), F32)
        return carry

    lax.fori_loop(0, LF * 2 * NC // LANES, clear, 0)
    to_scalar.wait()
    lane = iota((1, LANES), 1) & 7

    def add(i, carry):
        for e in range(CAP * K):
            code = index_s[i, e]
            line = values[i, e // 8 : e // 8 + 1, e % 8 * LANES : (e % 8 + 1) * LANES]
            field = fields[e % COPIES]
            field[pl.ds(shift(code, 3), 1), :] += jnp.where(lane == (code & 7), line, 0.0)
        return carry

    lax.fori_loop(0, BANDS, add, 0)

    def turn(f, carry):
        for half in range(2):
            for c in range(NC // LANES):
                rows = pl.ds((f * 2 + half) * NC + c * LANES, LANES)
                block = sum(field[rows, :] for field in fields)
                turned = block.T.reshape(LEV, 8, LANES)
                cols = slice(c * LANES, (c + 1) * LANES)
                value = dense[:, f, half * 8 : half * 8 + 8, cols] + turned
                out[:, f, half * 8 : half * 8 + 8, cols] = value
                if half == 0:
                    ups[:, f, :, cols] = cy[:, f, 0:8, cols] * value
        return carry

    lax.fori_loop(0, LF, turn, 0)
    west(out, cx, sides)


def last_kernel(a, cx, cy, ups, sides, out, below, side_in, rot, *sems):
    halo = Halo(ups, sides, below, side_in, rot, sems)
    barrier = pltpu.get_barrier_semaphore()
    expected = halo.greet(barrier)
    halo.zero()
    pl.semaphore_wait(barrier, expected)
    halo.start()
    interior(a, cx, cy, out, 0, LEV)
    halo.relay()
    halo.wait_rows()
    patch_rows(out, below, side_in)
    halo.wait_rotated()
    patch_rotated(out, rot)
    halo.finish()


def params(mib, cid=None):
    kw = {} if cid is None else dict(collective_id=cid, has_side_effects=True)
    return pltpu.CompilerParams(vmem_limit_bytes=mib * 1024 * 1024, **kw)


def per_device(final_adjoint, courant_x, courant_y, ray_tiles, ray_innov, ray_dest, ray_cols):
    vmem, anywhere = pl.BlockSpec(memory_space=pltpu.VMEM), pl.BlockSpec(memory_space=pl.ANY)
    field = jax.ShapeDtypeStruct(FIELD, F32)
    dma = pltpu.SemaphoreType.DMA
    dense, recv, held_x, held_y = pl.pallas_call(
        first_kernel,
        out_shape=(field, jax.ShapeDtypeStruct((BANDS, PACK, LANES), F32), field, field),
        in_specs=[pl.BlockSpec(memory_space=pltpu.HBM)] * 7,
        out_specs=(vmem, anywhere, vmem, vmem),
        scratch_shapes=[
            pltpu.VMEM(FIELD, F32),
            pltpu.VMEM((1, BANDS, RAYS, LEV * K), BF16),
            pltpu.VMEM((1, RAYS, BANDS), BF16),
            pltpu.VMEM((1, 1, BANDS), I32),
            pltpu.VMEM((1, K, BANDS), I32),
            pltpu.VMEM((BANDS, PACK, LANES), F32),
            dma((7,)), dma, dma, dma,
            pltpu.VMEM(UPS, F32),
            pltpu.VMEM(SIDES, F32),
        ] + halo_in(),
        compiler_params=params(28, 0),
        name="sums_and_first_step",
    )(*(
        pltpu.with_memory_space_constraint(value, pltpu.HBM)
        for value in (
            final_adjoint, courant_x, courant_y, ray_tiles,
            jnp.swapaxes(ray_innov, 1, 2), jnp.swapaxes(ray_dest, 1, 2), jnp.swapaxes(ray_cols, 1, 2),
        )
    ))
    mid, ups, sides = pl.pallas_call(
        scatter_kernel,
        out_shape=(field, jax.ShapeDtypeStruct(UPS, F32), jax.ShapeDtypeStruct(SIDES, F32)),
        in_specs=[vmem] * 4,
        out_specs=(vmem, vmem, vmem),
        scratch_shapes=[
            pltpu.VMEM((BANDS, LANES), I32),
            pltpu.SMEM((BANDS, LANES), I32),
            pltpu.VMEM((BANDS, CAP * 4, 8 * LANES), F32),
        ] + [pltpu.VMEM((LF * 2 * NC, LANES), F32)] * COPIES + [dma],
        compiler_params=params(36),
        name="forcing",
    )(recv, dense, held_x, held_y)
    return pl.pallas_call(
        last_kernel,
        out_shape=field,
        in_specs=[vmem] * 5,
        out_specs=vmem,
        scratch_shapes=halo_in(),
        compiler_params=params(28, 1),
        name="second_step",
    )(mid, held_x, held_y, ups, sides)


def solution(mesh):
    placed = (
        P(None, "face", "rows", None),
        P(None, "face", "rows", None),
        P(None, "face", "rows", None),
        P("face", "rows", None, None),
        P("face", "rows", None),
        P("face", "rows", None),
        P("face", "rows", None),
    )
    return jax.shard_map(
        per_device,
        mesh=mesh,
        in_specs=placed,
        out_specs=P(None, "face", "rows", None),
        check_vma=False,
    )
```

```python
import functools

import jax
import jax.numpy as jnp
from jax import lax
from jax.experimental import pallas as pl
from jax.experimental.pallas import tpu as pltpu
from jax.sharding import PartitionSpec as P

LEV, LF, RD, NC = 16, 3, 16, 1024
BANDS, RAYS, K, CAP = 64, 16, 32, 2
GROUP = 8
RELAYS = BANDS // GROUP
LANES = 128
PACK = 16
SENT = 9
F32, BF16, I32 = jnp.float32, jnp.bfloat16, jnp.int32
MESH = pl.DeviceIdType.MESH


def iota(shape, dim):
    return lax.broadcasted_iota(I32, shape, dim)


def dot(a, b):
    return jnp.dot(a, b, preferred_element_type=F32)


def dot_t(a, b):
    return lax.dot_general(a, b, (((1,), (1,)), ((), ())), preferred_element_type=F32)


def split(value):
    high = value.astype(BF16)
    rest = value - high.astype(F32)
    mid = rest.astype(BF16)
    return high, mid, rest - mid.astype(F32)


class Halo:
    def __init__(self, ups, sides, seam, below, side_in, rot, sems):
        self.ups, self.sides, self.seam, self.below, self.side_in, self.rot = ups, sides, seam, below, side_in, rot
        self.send, self.recv, self.rot_send, self.fwd_send, self.rot_recv = sems
        self.g = lax.axis_index("face")
        self.b = lax.axis_index("rows")

    def greet(self, barrier):
        g, b = self.g, self.b

        def hello(face, band):
            pl.semaphore_signal(barrier, inc=1, device_id=(face, band), device_id_type=MESH)

        hello(1 - g, b)

        @pl.when(b < BANDS - 1)
        def _():
            hello(g, b + 1)

        @pl.when(b == BANDS - 1)
        def _():
            hello(g, 0)

        @pl.when((b == BANDS - 1) & (g == 0))
        def _():
            hello(1, 0)

        @pl.when((b & (GROUP - 1)) != 0)
        def _():
            hello(g, b & -GROUP)

        @pl.when((b & (GROUP - 1)) == 0)
        def _():
            hello(1 - g, 0)

        @pl.when(((b & (GROUP - 1)) == 0) & (g == 0) & (b != 0))
        def _():
            hello(0, 0)

        relay = ((b & (GROUP - 1)) == 0).astype(I32)
        origin = (b == 0).astype(I32)
        return 2 + relay * (GROUP - 1) + origin * (RELAYS + jnp.where(g == 0, RELAYS - 1, 1))

    def zero(self):
        g, b = self.g, self.b
        edge = jnp.zeros((LEV, 1, NC), F32)

        @pl.when(b == BANDS - 1)
        def _():
            @pl.when(g == 0)
            def _():
                self.below[:, 1] = edge

            @pl.when(g == 1)
            def _():
                self.below[:, 0] = edge
                self.below[:, 2] = edge

        @pl.when(g == 1)
        def _():
            self.rot[1] = jnp.zeros((LEV, LANES), F32)

    def copy(self, src, dst, send, recv, face, band):
        return pltpu.make_async_remote_copy(
            src_ref=src, dst_ref=dst, send_sem=send, recv_sem=recv,
            device_id=(face, band), device_id_type=MESH,
        )

    def row(self, face):
        return self.copy(self.ups.at[:, :, 0:1, :], self.below, self.send.at[0], self.recv.at[0], self.g, face)

    def one(self, src, dst, face, slot):
        return self.copy(
            self.ups.at[:, src, 0:1, :], self.below.at[:, dst], self.send.at[slot], self.recv.at[slot], face, BANDS - 1
        )

    def side(self):
        return self.copy(self.sides, self.side_in, self.send.at[1], self.recv.at[1], 1 - self.g, self.b)

    def piece(self, which, face, r, n):
        lanes = pl.ds(LANES * (RELAYS - 1 - r), LANES)
        return self.copy(
            self.seam.at[which, :, lanes], self.rot.at[which],
            self.rot_send.at[which, r], self.rot_recv.at[which], face, n,
        )

    def start(self):
        g, b = self.g, self.b

        @pl.when(b == 0)
        def _():
            @pl.when(g == 0)
            def _():
                for l in range(LEV):
                    self.seam[0, l : l + 1, :] = self.ups[l, 2, 0:1, :]
                    self.seam[1, l : l + 1, :] = self.ups[l, 0, 0:1, :]
                for r in range(RELAYS):
                    self.piece(0, 1, r, r * GROUP).start()
                for r in range(1, RELAYS):
                    self.piece(1, 0, r, r * GROUP).start()
                self.one(1, 2, 0, 0).start()
                self.rot[1] = self.seam[1, :, NC - LANES :]

            @pl.when(g == 1)
            def _():
                for l in range(LEV):
                    self.seam[0, l : l + 1, :] = self.ups[l, 1, 0:1, :]
                for r in range(RELAYS):
                    self.piece(0, 0, r, r * GROUP).start()
                self.one(0, 1, 1, 0).start()
                self.one(2, 0, 0, 2).start()

        @pl.when(b != 0)
        def _():
            self.row(b - 1).start()

    def forward(self, dst, i):
        return self.copy(
            self.rot.at[dst], self.rot.at[dst], self.fwd_send.at[dst, i], self.rot_recv.at[dst],
            self.g, (self.b & -GROUP) + i,
        )

    def relay(self):
        g, b = self.g, self.b

        @pl.when((b & (GROUP - 1)) == 0)
        def _():
            self.forward(0, 1).wait_recv()
            for i in range(1, GROUP):
                self.forward(0, i).start()

            @pl.when(g == 0)
            def _():
                @pl.when(b != 0)
                def _():
                    self.forward(1, 1).wait_recv()

                for i in range(1, GROUP):
                    self.forward(1, i).start()

    def wait_rotated(self):
        g, b = self.g, self.b

        @pl.when((b & (GROUP - 1)) != 0)
        def _():
            self.forward(0, 1).wait_recv()

            @pl.when(g == 0)
            def _():
                self.forward(1, 1).wait_recv()

    def wait_rows(self):
        g, b = self.g, self.b

        @pl.when(b != BANDS - 1)
        def _():
            self.row(0).wait_recv()

        @pl.when(b == BANDS - 1)
        def _():
            @pl.when(g == 0)
            def _():
                self.one(1, 2, 0, 0).wait_recv()
                self.one(2, 0, 0, 2).wait_recv()

            @pl.when(g == 1)
            def _():
                self.one(0, 1, 1, 0).wait_recv()

    def finish(self):
        g, b = self.g, self.b
        self.side().wait_send()

        @pl.when(b != 0)
        def _():
            self.row(0).wait_send()

        @pl.when(b == 0)
        def _():
            @pl.when(g == 0)
            def _():
                for r in range(RELAYS):
                    self.piece(0, 1, r, r * GROUP).wait_send()
                for r in range(1, RELAYS):
                    self.piece(1, 0, r, r * GROUP).wait_send()
                self.one(1, 2, 0, 0).wait_send()

            @pl.when(g == 1)
            def _():
                for r in range(RELAYS):
                    self.piece(0, 0, r, r * GROUP).wait_send()
                self.one(0, 1, 1, 0).wait_send()
                self.one(2, 0, 0, 2).wait_send()

        @pl.when((b & (GROUP - 1)) == 0)
        def _():
            for i in range(1, GROUP):
                self.forward(0, i).wait_send()

            @pl.when(g == 0)
            def _():
                for i in range(1, GROUP):
                    self.forward(1, i).wait_send()


def landing():
    return [
        (LEV, LF, 1, NC),
        (RD, LANES),
        (2, LEV, LANES),
    ]


def halo_scratch():
    return [
        pltpu.VMEM(UPS, F32),
        pltpu.VMEM(SIDES, F32),
        pltpu.VMEM((2, LEV, NC), F32),
        pltpu.SemaphoreType.DMA((3,)),
        pltpu.SemaphoreType.DMA((3,)),
        pltpu.SemaphoreType.DMA((2, RELAYS)),
        pltpu.SemaphoreType.DMA((2, GROUP)),
        pltpu.SemaphoreType.DMA((2,)),
    ]


UPS = (LEV, LF, 8, NC)
SIDES = (RD, LANES)
FIELD = (LEV, LF, RD, NC)


def west(along, sides):
    lane = iota(SIDES, 1)
    total = jnp.zeros(SIDES, F32)
    for l in range(LEV):
        total = jnp.where(lane == l, jnp.broadcast_to(along[l, :, 0:1], SIDES), total)
    sides[...] = total


def interior(a, cx, cy, out, lo, hi):
    row = iota((RD, NC), 0)
    col = iota((RD, NC), 1)

    def body(l, carry):
        base, rolled = [], []
        for f in range(LF):
            value, x, y = a[l, f], cx[l, f], cy[l, f]
            along, upward = x * value, y * value
            rolled.append(pltpu.roll(along, NC - 1, 1))
            lifted = jnp.where(row < RD - 1, pltpu.roll(upward, RD - 1, 0), 0.0)
            base.append((1.0 - x - y) * value + lifted)
        for f in range(LF):
            beyond = rolled[f + 1] if f + 1 < LF else 0.0
            out[l, f] = base[f] + jnp.where(col < NC - 1, rolled[f], beyond)
        return carry

    lax.fori_loop(lo, hi, body, 0)


def patch_rows(out, below, side_in, lo, hi):
    def body(l, carry):
        for f in range(LF):
            out[l, f, RD - 1 : RD, :] += below[l, f]
        return carry

    lax.fori_loop(lo, hi, body, 0)
    full = (hi - lo, RD, LANES)
    lane = iota(full, 2)
    mine = jnp.where(lane == iota(full, 0) + lo, jnp.broadcast_to(side_in[...][None], full), 0.0)
    right = jnp.sum(mine, axis=2, keepdims=True)
    out[lo:hi, 2, :, NC - LANES :] += jnp.where(lane == LANES - 1, right, 0.0)


def patch_rotated(out, rot, lo, hi):
    g = lax.axis_index("face")
    b = lax.axis_index("rows")
    full = (hi - lo, RD, LANES)
    lane = iota(full, 2)
    place = LANES - 1 - RD * (b & (GROUP - 1)) - iota(full, 1)

    def column(which):
        piece = rot[which, lo:hi, :]
        picked = jnp.where(lane == place, jnp.broadcast_to(piece[:, None, :], full), 0.0)
        return jnp.where(lane == 0, jnp.sum(picked, axis=2, keepdims=True), 0.0)

    out[lo:hi, pl.ds(g, 1), :, 0:LANES] += column(0).reshape(hi - lo, 1, RD, LANES)

    @pl.when(g == 0)
    def _():
        out[lo:hi, 2, :, 0:LANES] += column(1)


def pack(tiles, innov, dest, cells, send):
    blocks = BANDS
    wide = blocks * RAYS
    ray = iota((RAYS, wide), 1) & (RAYS - 1)
    repeat = (lax.shift_right_logical(iota((blocks, wide), 1), 4) == iota((blocks, wide), 0)).astype(BF16)
    lines = jnp.where(ray == iota((RAYS, wide), 0), dot(innov[0], repeat), 0.0)
    weight = jnp.sum(lines, axis=0, keepdims=True)

    square = (blocks, blocks)
    first, second = iota(square, 0), iota(square, 1)
    target = jnp.broadcast_to(dest[0].astype(F32), square)
    other = dot(jnp.where(first == second, target, 0.0).astype(BF16), jnp.ones(square, BF16))
    same = (other == target) & (first < second)
    order = jnp.sum(same.astype(F32), axis=0, keepdims=True)
    slot = iota((CAP * BANDS, blocks), 0)
    band = ((slot + lax.axis_index("rows")) & (BANDS - 1)).astype(F32)
    turn = lax.shift_right_logical(slot, 6).astype(F32)
    chosen = ((band == target[0:1]) & (turn == order)).astype(BF16)

    sums = dot((dot(chosen, repeat) * weight).astype(BF16), tiles[0].reshape(wide, LEV * K))
    src, dst = iota((LEV * K, LEV * K), 0), iota((LEV * K, LEV * K), 1)
    inner = lax.shift_right_logical(dst & (LANES - 1), 4)
    part = lax.shift_right_logical(dst, 7)
    mixed = (src == (dst & (LEV - 1)) * K + part * 8 + inner).astype(BF16)
    high, mid, low = split(sums)
    sums = dot(high, mixed) + dot(mid, mixed) + dot(low.astype(BF16), mixed)

    cell = cells[0]
    upper = lax.shift_right_logical(cell, 8).astype(F32).astype(BF16)
    lower = (cell & 255).astype(F32).astype(BF16)
    codes = dot_t(chosen, upper) * 256.0 + dot_t(chosen, lower)
    codes = jnp.concatenate(
        [codes[:BANDS], codes[BANDS:], jnp.zeros((BANDS, LANES - 2 * K), F32)], axis=1
    )
    flat = send.reshape(BANDS * PACK, LANES)
    for s in range(CAP):
        for q in range(4):
            flat[pl.ds(s * 4 + q, BANDS, stride=PACK), :] = sums[
                s * BANDS : (s + 1) * BANDS, q * LANES : (q + 1) * LANES
            ]
    flat[pl.ds(SENT - 1, BANDS, stride=PACK), :] = codes


HALF = BANDS // 2
DEPTH = HALF * CAP * K
WIDE = 256


def one_hots(recv, first, left, right, top):
    flat = recv.reshape(BANDS * PACK, LANES)
    at = first * PACK
    codes = flat[pl.ds(at + SENT - 1, HALF, stride=PACK), :]
    face_row = iota((LF * RD, LANES), 0)
    column = iota((LANES, NC), 1)
    size = LEV * LF * RD
    for pair in range(2):
        spots = [(s, 2 * pair + half) for half in range(2) for s in range(CAP)]
        sums = jnp.concatenate(
            [flat[pl.ds(at + s * 4 + q, HALF, stride=PACK), :] for s, q in spots], axis=0
        ).T
        cells = jnp.concatenate(
            [pltpu.roll(codes, (LANES - s * K - q * 8) % LANES, 1) for s, q in spots], axis=0
        )
        rows = lax.shift_right_logical(cells.T.astype(I32), 10)
        cols = cells.astype(I32) & (NC - 1)
        for inner in range(8):
            part = slice((pair * 8 + inner) * LANES, (pair * 8 + inner + 1) * LANES)
            high, mid, _ = split(sums[inner * LEV : (inner + 1) * LEV])
            row = rows[inner : inner + 1]
            chosen = jnp.where(face_row == row, 1.0, 0.0).astype(BF16)
            for n, term in enumerate((high, mid)):
                product = term[:, None, :] * chosen[None]
                left[n * size : (n + 1) * size, part] = product.reshape(size, LANES)
                if top is not None:
                    for f in range(LF):
                        kept = jnp.where(row == f * RD, term.astype(F32), 0.0).astype(BF16)
                        top[(n * LF + f) * LEV : (n * LF + f + 1) * LEV, part] = kept
            right[part, :] = jnp.where(column == cols[:, inner : inner + 1], 1.0, 0.0).astype(BF16)


def add_product(left, right, out, lo, hi):
    size = LEV * LF * RD

    def body(n, carry):
        cols = pl.ds(pl.multiple_of(n * WIDE, WIDE), WIDE)
        both = dot(left[...], right[:, cols])
        out[:, :, :, cols] += (both[:size] + both[size:]).reshape(LEV, LF, RD, WIDE)
        return carry

    lax.fori_loop(lo, hi, body, 0)


def first_kernel(
    a_hbm, cx_hbm, cy_hbm, tiles_hbm, innov_hbm, dest_hbm, cells_hbm,
    out, cx, cy, below2, side_in2, rot2,
    a, tiles, innov, dest, cells, send, recv, left, right, top, load_sem, pack_send, pack_recv, own_sem,
    below, side_in, rot, ups, sides, seam, sem1, sem2, sem3, sem4, sem5,
    ups2, sides2, seam2, *sems2,
):
    g = lax.axis_index("face")
    b = lax.axis_index("rows")
    pairs = (
        (innov_hbm, innov), (dest_hbm, dest), (cells_hbm, cells), (tiles_hbm, tiles),
        (a_hbm, a), (cy_hbm, cy), (cx_hbm, cx),
    )
    loads = [pltpu.make_async_copy(src, dst, load_sem.at[i]) for i, (src, dst) in enumerate(pairs)]
    for load in loads:
        load.start()
    halo = Halo(ups, sides, seam, below, side_in, rot, (sem1, sem2, sem3, sem4, sem5))
    halo2 = Halo(ups2, sides2, seam2, below2, side_in2, rot2, sems2)
    barrier = pltpu.get_barrier_semaphore()
    expected = halo.greet(barrier) + BANDS - 1

    def hello(i, carry):
        pl.semaphore_signal(barrier, inc=1, device_id=(g, (b + i) & (BANDS - 1)), device_id_type=MESH)
        return carry

    lax.fori_loop(1, BANDS, hello, 0)
    halo.zero()
    halo2.zero()
    for load in loads[:4]:
        load.wait()
    pack(tiles, innov, dest, cells, send)
    own = pltpu.make_async_copy(send.at[0, pl.ds(0, SENT)], recv.at[0, pl.ds(0, SENT)], own_sem)
    own.start()
    for load in loads[4:]:
        load.wait()

    def lift(l, carry):
        ups[l] = cy[l, :, 0:8, :] * a[l, :, 0:8, :]
        return carry

    lax.fori_loop(0, LEV, lift, 0)
    west(cx[:, 0, :, 0:LANES] * a[:, 0, :, 0:LANES], sides)
    pl.semaphore_wait(barrier, expected)
    halo.start()
    halo.side().start()

    def packets(which, half, band):
        return pltpu.make_async_remote_copy(
            src_ref=send.at[which, pl.ds(0, SENT)],
            dst_ref=recv.at[which, pl.ds(0, SENT)],
            send_sem=pack_send,
            recv_sem=pack_recv.at[half],
            device_id=(g, band),
            device_id_type=MESH,
        )

    for half in range(2):

        def ship(i, carry, half=half):
            packets(i, half, (b + i) & (BANDS - 1)).start()
            return carry

        lax.fori_loop(max(1, half * HALF), (half + 1) * HALF, ship, 0)
    halo.relay()
    interior(a, cx, cy, out, 0, LEV)
    own.wait()
    packets(pl.ds(1, HALF - 1), 0, b).wait_recv()
    one_hots(recv, 0, left, right, None)
    add_product(left, right, out, 0, NC // WIDE)
    halo.wait_rows()
    halo.side().wait_recv()
    patch_rows(out, below, side_in, 0, LEV)
    halo.wait_rotated()
    patch_rotated(out, rot, 0, LEV)
    packets(pl.ds(HALF, HALF), 1, b).wait_recv()
    one_hots(recv, HALF, left, right, top)
    first = dot(top[...], right[...])
    first = first[: LF * LEV] + first[LF * LEV :]
    for l in range(LEV):
        for f in range(LF):
            value = out[l, f, 0:1, :] + first[f * LEV + l : f * LEV + l + 1]
            ups2[l, f, 0:1, :] = cy[l, f, 0:1, :] * value
    halo2.start()
    add_product(left, right, out, 0, 1)
    west(cx[:, 0, :, 0:LANES] * out[:, 0, :, 0:LANES], sides2)
    halo2.side().start()
    add_product(left, right, out, 1, 2)
    halo2.relay()
    add_product(left, right, out, 2, NC // WIDE)
    halo2.wait_rows()
    halo2.side().wait_recv()
    halo2.wait_rotated()
    halo.finish()
    halo2.finish()
    packets(pl.ds(1, BANDS - 1), 0, b).wait_send()


PARTS = 4


def last_kernel(a, cx, cy, below, side_in, rot, out_hbm, out, sems):
    step = LEV // PARTS
    copies = []
    for p in range(PARTS):
        lo, hi = p * step, (p + 1) * step
        interior(a, cx, cy, out, lo, hi)
        patch_rows(out, below, side_in, lo, hi)
        patch_rotated(out, rot, lo, hi)
        copies.append(pltpu.make_async_copy(out.at[lo:hi], out_hbm.at[lo:hi], sems.at[p]))
        copies[-1].start()
    for copy in copies:
        copy.wait()


def params(mib, cid=None):
    kw = {} if cid is None else dict(collective_id=cid, has_side_effects=True)
    return pltpu.CompilerParams(vmem_limit_bytes=mib * 1024 * 1024, **kw)


def per_device(final_adjoint, courant_x, courant_y, ray_tiles, ray_innov, ray_dest, ray_cols):
    vmem, anywhere = pl.BlockSpec(memory_space=pltpu.VMEM), pl.BlockSpec(memory_space=pl.ANY)
    field = jax.ShapeDtypeStruct(FIELD, F32)
    dma = pltpu.SemaphoreType.DMA
    size = LEV * LF * RD
    mid, held_x, held_y, below, side_in, rot = pl.pallas_call(
        first_kernel,
        out_shape=[field] * 3 + [jax.ShapeDtypeStruct(shape, F32) for shape in landing()],
        in_specs=[anywhere] * 7,
        out_specs=[vmem] * 6,
        scratch_shapes=[
            pltpu.VMEM(FIELD, F32),
            pltpu.VMEM((1, BANDS, RAYS, LEV * K), BF16),
            pltpu.VMEM((1, RAYS, BANDS), BF16),
            pltpu.VMEM((1, 1, BANDS), I32),
            pltpu.VMEM((1, K, BANDS), I32),
            pltpu.VMEM((BANDS, PACK, LANES), F32),
            pltpu.VMEM((BANDS, PACK, LANES), F32),
            pltpu.VMEM((2 * size, DEPTH), BF16),
            pltpu.VMEM((DEPTH, NC), BF16),
            pltpu.VMEM((2 * LF * LEV, DEPTH), BF16),
            dma((7,)), dma, dma((2,)), dma,
        ] + [pltpu.VMEM(shape, F32) for shape in landing()] + halo_scratch() + halo_scratch(),
        compiler_params=params(40, 0),
        name="sums_and_adjoint",
    )(*(
        pltpu.with_memory_space_constraint(value, pltpu.HBM)
        for value in (
            final_adjoint, courant_x, courant_y, ray_tiles,
            jnp.swapaxes(ray_innov, 1, 2), jnp.swapaxes(ray_dest, 1, 2), jnp.swapaxes(ray_cols, 1, 2),
        )
    ))
    return pl.pallas_call(
        last_kernel,
        out_shape=field,
        in_specs=[vmem] * 6,
        out_specs=anywhere,
        scratch_shapes=[pltpu.VMEM(FIELD, F32), dma((PARTS,))],
        compiler_params=params(24),
        name="second_step",
    )(mid, held_x, held_y, below, side_in, rot)


def solution(mesh):
    placed = (
        P(None, "face", "rows", None),
        P(None, "face", "rows", None),
        P(None, "face", "rows", None),
        P("face", "rows", None, None),
        P("face", "rows", None),
        P("face", "rows", None),
        P("face", "rows", None),
    )
    return jax.shard_map(
        per_device,
        mesh=mesh,
        in_specs=placed,
        out_specs=P(None, "face", "rows", None),
        check_vma=False,
    )
```

```python
import functools

import jax
import jax.numpy as jnp
from jax import lax
from jax.experimental import pallas as pl
from jax.experimental.pallas import tpu as pltpu
from jax.sharding import PartitionSpec as P

LEV, LF, RD, NC = 16, 3, 16, 1024
BANDS, RAYS, K, CAP = 64, 16, 32, 2
GROUP = 8
RELAYS = BANDS // GROUP
LANES = 128
PACK = 16
SENT = 9
F32, BF16, I32 = jnp.float32, jnp.bfloat16, jnp.int32
MESH = pl.DeviceIdType.MESH


def iota(shape, dim):
    return lax.broadcasted_iota(I32, shape, dim)


def dot(a, b):
    return jnp.dot(a, b, preferred_element_type=F32)


def dot_t(a, b):
    return lax.dot_general(a, b, (((1,), (1,)), ((), ())), preferred_element_type=F32)


def split(value):
    high = value.astype(BF16)
    rest = value - high.astype(F32)
    mid = rest.astype(BF16)
    return high, mid, rest - mid.astype(F32)


class Halo:
    def __init__(self, ups, sides, seam, below, side_in, rot, sems):
        self.ups, self.sides, self.seam, self.below, self.side_in, self.rot = ups, sides, seam, below, side_in, rot
        self.send, self.recv, self.rot_send, self.fwd_send, self.rot_recv = sems
        self.g = lax.axis_index("face")
        self.b = lax.axis_index("rows")

    def greet(self, barrier):
        g, b = self.g, self.b

        def hello(face, band):
            pl.semaphore_signal(barrier, inc=1, device_id=(face, band), device_id_type=MESH)

        hello(1 - g, b)

        @pl.when(b < BANDS - 1)
        def _():
            hello(g, b + 1)

        @pl.when(b == BANDS - 1)
        def _():
            hello(g, 0)

        @pl.when((b == BANDS - 1) & (g == 0))
        def _():
            hello(1, 0)

        @pl.when((b & (GROUP - 1)) != 0)
        def _():
            hello(g, b & -GROUP)

        @pl.when((b & (GROUP - 1)) == 0)
        def _():
            hello(1 - g, 0)

        @pl.when(((b & (GROUP - 1)) == 0) & (g == 0) & (b != 0))
        def _():
            hello(0, 0)

        relay = ((b & (GROUP - 1)) == 0).astype(I32)
        origin = (b == 0).astype(I32)
        return 2 + relay * (GROUP - 1) + origin * (RELAYS + jnp.where(g == 0, RELAYS - 1, 1))

    def zero(self):
        g, b = self.g, self.b
        edge = jnp.zeros((LEV, 1, NC), F32)

        @pl.when(b == BANDS - 1)
        def _():
            @pl.when(g == 0)
            def _():
                self.below[:, 1] = edge

            @pl.when(g == 1)
            def _():
                self.below[:, 0] = edge
                self.below[:, 2] = edge

        @pl.when(g == 1)
        def _():
            self.rot[1] = jnp.zeros((LEV, LANES), F32)

    def copy(self, src, dst, send, recv, face, band):
        return pltpu.make_async_remote_copy(
            src_ref=src, dst_ref=dst, send_sem=send, recv_sem=recv,
            device_id=(face, band), device_id_type=MESH,
        )

    def row(self, face):
        return self.copy(self.ups.at[:, :, 0:1, :], self.below, self.send.at[0], self.recv.at[0], self.g, face)

    def one(self, src, dst, face, slot):
        return self.copy(
            self.ups.at[:, src, 0:1, :], self.below.at[:, dst], self.send.at[slot], self.recv.at[slot], face, BANDS - 1
        )

    def side(self):
        return self.copy(self.sides, self.side_in, self.send.at[1], self.recv.at[1], 1 - self.g, self.b)

    def piece(self, which, face, r, n):
        lanes = pl.ds(LANES * (RELAYS - 1 - r), LANES)
        return self.copy(
            self.seam.at[which, :, lanes], self.rot.at[which],
            self.rot_send.at[which, r], self.rot_recv.at[which], face, n,
        )

    def start_rotated(self):
        g, b = self.g, self.b

        @pl.when(b == 0)
        def _():
            @pl.when(g == 0)
            def _():
                for l in range(LEV):
                    self.seam[0, l : l + 1, :] = self.ups[l, 2, 0:1, :]
                    self.seam[1, l : l + 1, :] = self.ups[l, 0, 0:1, :]
                for r in range(RELAYS):
                    self.piece(0, 1, r, r * GROUP).start()
                for r in range(1, RELAYS):
                    self.piece(1, 0, r, r * GROUP).start()
                self.rot[1] = self.seam[1, :, NC - LANES :]

            @pl.when(g == 1)
            def _():
                for l in range(LEV):
                    self.seam[0, l : l + 1, :] = self.ups[l, 1, 0:1, :]
                for r in range(RELAYS):
                    self.piece(0, 0, r, r * GROUP).start()

    def start_rows(self):
        g, b = self.g, self.b

        @pl.when(b == 0)
        def _():
            @pl.when(g == 0)
            def _():
                self.one(1, 2, 0, 0).start()

            @pl.when(g == 1)
            def _():
                self.one(0, 1, 1, 0).start()
                self.one(2, 0, 0, 2).start()

        @pl.when(b != 0)
        def _():
            self.row(b - 1).start()

    def forward(self, dst, i):
        return self.copy(
            self.rot.at[dst], self.rot.at[dst], self.fwd_send.at[dst, i], self.rot_recv.at[dst],
            self.g, (self.b & -GROUP) + i,
        )

    def relay(self):
        g, b = self.g, self.b

        @pl.when((b & (GROUP - 1)) == 0)
        def _():
            self.forward(0, 1).wait_recv()
            for i in range(1, GROUP):
                self.forward(0, i).start()

            @pl.when(g == 0)
            def _():
                @pl.when(b != 0)
                def _():
                    self.forward(1, 1).wait_recv()

                for i in range(1, GROUP):
                    self.forward(1, i).start()

    def wait_rotated(self):
        g, b = self.g, self.b

        @pl.when((b & (GROUP - 1)) != 0)
        def _():
            self.forward(0, 1).wait_recv()

            @pl.when(g == 0)
            def _():
                self.forward(1, 1).wait_recv()

    def wait_rows(self):
        g, b = self.g, self.b

        @pl.when(b != BANDS - 1)
        def _():
            self.row(0).wait_recv()

        @pl.when(b == BANDS - 1)
        def _():
            @pl.when(g == 0)
            def _():
                self.one(1, 2, 0, 0).wait_recv()
                self.one(2, 0, 0, 2).wait_recv()

            @pl.when(g == 1)
            def _():
                self.one(0, 1, 1, 0).wait_recv()

    def finish(self):
        g, b = self.g, self.b
        self.side().wait_send()

        @pl.when(b != 0)
        def _():
            self.row(0).wait_send()

        @pl.when(b == 0)
        def _():
            @pl.when(g == 0)
            def _():
                for r in range(RELAYS):
                    self.piece(0, 1, r, r * GROUP).wait_send()
                for r in range(1, RELAYS):
                    self.piece(1, 0, r, r * GROUP).wait_send()
                self.one(1, 2, 0, 0).wait_send()

            @pl.when(g == 1)
            def _():
                for r in range(RELAYS):
                    self.piece(0, 0, r, r * GROUP).wait_send()
                self.one(0, 1, 1, 0).wait_send()
                self.one(2, 0, 0, 2).wait_send()

        @pl.when((b & (GROUP - 1)) == 0)
        def _():
            for i in range(1, GROUP):
                self.forward(0, i).wait_send()

            @pl.when(g == 0)
            def _():
                for i in range(1, GROUP):
                    self.forward(1, i).wait_send()


def landing():
    return [
        (LEV, LF, 1, NC),
        (RD, LANES),
        (2, LEV, LANES),
    ]


def halo_scratch():
    return [
        pltpu.VMEM(UPS, F32),
        pltpu.VMEM(SIDES, F32),
        pltpu.VMEM((2, LEV, NC), F32),
        pltpu.SemaphoreType.DMA((3,)),
        pltpu.SemaphoreType.DMA((3,)),
        pltpu.SemaphoreType.DMA((2, RELAYS)),
        pltpu.SemaphoreType.DMA((2, GROUP)),
        pltpu.SemaphoreType.DMA((2,)),
    ]


UPS = (LEV, LF, 8, NC)
SIDES = (RD, LANES)
FIELD = (LEV, LF, RD, NC)


def west(along, sides):
    lane = iota(SIDES, 1)
    total = jnp.zeros(SIDES, F32)
    for l in range(LEV):
        total = jnp.where(lane == l, jnp.broadcast_to(along[l, :, 0:1], SIDES), total)
    sides[...] = total


def interior(a, cx, cy, out, lo, hi):
    row = iota((RD, NC), 0)
    col = iota((RD, NC), 1)

    def body(l, carry):
        base, rolled = [], []
        for f in range(LF):
            value, x, y = a[l, f], cx[l, f], cy[l, f]
            along, upward = x * value, y * value
            rolled.append(pltpu.roll(along, NC - 1, 1))
            lifted = jnp.where(row < RD - 1, pltpu.roll(upward, RD - 1, 0), 0.0)
            base.append((1.0 - x - y) * value + lifted)
        for f in range(LF):
            beyond = rolled[f + 1] if f + 1 < LF else 0.0
            out[l, f] = base[f] + jnp.where(col < NC - 1, rolled[f], beyond)
        return carry

    lax.fori_loop(lo, hi, body, 0)


def patch_rows(out, below, lo, hi):
    def body(l, carry):
        for f in range(LF):
            out[l, f, RD - 1 : RD, :] += below[l, f]
        return carry

    lax.fori_loop(lo, hi, body, 0)


def patch_west(out, side_in, lo, hi):
    full = (hi - lo, RD, LANES)
    lane = iota(full, 2)
    mine = jnp.where(lane == iota(full, 0) + lo, jnp.broadcast_to(side_in[...][None], full), 0.0)
    right = jnp.sum(mine, axis=2, keepdims=True)
    out[lo:hi, 2, :, NC - LANES :] += jnp.where(lane == LANES - 1, right, 0.0)


def patch_rotated(out, rot, lo, hi):
    g = lax.axis_index("face")
    b = lax.axis_index("rows")
    full = (hi - lo, RD, LANES)
    lane = iota(full, 2)
    place = LANES - 1 - RD * (b & (GROUP - 1)) - iota(full, 1)

    def column(which):
        piece = rot[which, lo:hi, :]
        picked = jnp.where(lane == place, jnp.broadcast_to(piece[:, None, :], full), 0.0)
        return jnp.where(lane == 0, jnp.sum(picked, axis=2, keepdims=True), 0.0)

    out[lo:hi, pl.ds(g, 1), :, 0:LANES] += column(0).reshape(hi - lo, 1, RD, LANES)

    @pl.when(g == 0)
    def _():
        out[lo:hi, 2, :, 0:LANES] += column(1)


def pack(tiles, innov, dest, cells, send):
    blocks = BANDS
    wide = blocks * RAYS
    ray = iota((RAYS, wide), 1) & (RAYS - 1)
    repeat = (lax.shift_right_logical(iota((blocks, wide), 1), 4) == iota((blocks, wide), 0)).astype(BF16)
    lines = jnp.where(ray == iota((RAYS, wide), 0), dot(innov[0], repeat), 0.0)
    weight = jnp.sum(lines, axis=0, keepdims=True)

    square = (blocks, blocks)
    first, second = iota(square, 0), iota(square, 1)
    target = jnp.broadcast_to(dest[0].astype(F32), square)
    other = dot(jnp.where(first == second, target, 0.0).astype(BF16), jnp.ones(square, BF16))
    same = (other == target) & (first < second)
    order = jnp.sum(same.astype(F32), axis=0, keepdims=True)
    slot = iota((CAP * BANDS, blocks), 0)
    band = ((slot + lax.axis_index("rows")) & (BANDS - 1)).astype(F32)
    turn = lax.shift_right_logical(slot, 6).astype(F32)
    chosen = ((band == target[0:1]) & (turn == order)).astype(BF16)

    sums = dot((dot(chosen, repeat) * weight).astype(BF16), tiles[0].reshape(wide, LEV * K))
    src, dst = iota((LEV * K, LEV * K), 0), iota((LEV * K, LEV * K), 1)
    inner = lax.shift_right_logical(dst & (LANES - 1), 4)
    part = lax.shift_right_logical(dst, 7)
    mixed = (src == (dst & (LEV - 1)) * K + part * 8 + inner).astype(BF16)
    high, mid, low = split(sums)
    sums = dot(high, mixed) + dot(mid, mixed) + dot(low.astype(BF16), mixed)

    cell = cells[0]
    upper = lax.shift_right_logical(cell, 8).astype(F32).astype(BF16)
    lower = (cell & 255).astype(F32).astype(BF16)
    codes = dot_t(chosen, upper) * 256.0 + dot_t(chosen, lower)
    codes = jnp.concatenate(
        [codes[:BANDS], codes[BANDS:], jnp.zeros((BANDS, LANES - 2 * K), F32)], axis=1
    )
    flat = send.reshape(BANDS * PACK, LANES)
    for s in range(CAP):
        for q in range(4):
            flat[pl.ds(s * 4 + q, BANDS, stride=PACK), :] = sums[
                s * BANDS : (s + 1) * BANDS, q * LANES : (q + 1) * LANES
            ]
    flat[pl.ds(SENT - 1, BANDS, stride=PACK), :] = codes


HALF = BANDS // 2
DEPTH = HALF * CAP * K
COPIES = 4


def factors(recv, first, right, top, spot, plain):
    flat = recv.reshape(BANDS * PACK, LANES)
    at = first * PACK
    codes = flat[pl.ds(at + SENT - 1, HALF, stride=PACK), :]
    column = iota((LANES, NC), 1)
    spot_row = iota((RD, LANES), 0)
    for pair in range(2):
        spots = [(s, 2 * pair + half) for half in range(2) for s in range(CAP)]
        sums = jnp.concatenate(
            [flat[pl.ds(at + s * 4 + q, HALF, stride=PACK), :] for s, q in spots], axis=0
        ).T
        cells = jnp.concatenate(
            [pltpu.roll(codes, (LANES - s * K - q * 8) % LANES, 1) for s, q in spots], axis=0
        )
        turned = cells.T.astype(I32)
        rows = lax.shift_right_logical(turned, 10)
        edge = jnp.where((turned & (NC - 1)) == 0, rows, LF * RD)
        cols = cells.astype(I32) & (NC - 1)
        for inner in range(8):
            part = slice((pair * 8 + inner) * LANES, (pair * 8 + inner + 1) * LANES)
            high, mid, _ = split(sums[inner * LEV : (inner + 1) * LEV])
            row = rows[inner : inner + 1]
            for n, term in enumerate((high, mid)):
                plain[n * LEV : (n + 1) * LEV, part] = term
                for f in range(LF):
                    kept = jnp.where(row == f * RD, term.astype(F32), 0.0).astype(BF16)
                    top[(n * LF + f) * LEV : (n * LF + f + 1) * LEV, part] = kept
            spot[:, part] = jnp.where(spot_row == edge[inner : inner + 1], 1.0, 0.0).astype(BF16)
            right[part, :] = jnp.where(column == cols[:, inner : inner + 1], 1.0, 0.0).astype(BF16)


def first_kernel(
    a_hbm, cx_hbm, cy_hbm, tiles_hbm, innov_hbm, dest_hbm, cells_hbm,
    out, cx, cy, values, index, below2, side_in2, rot2,
    a, tiles, innov, dest, cells, send, recv, right, top, spot, plain, sides_x, load_sem, pack_send, pack_recv, own_sem,
    below, side_in, rot, ups, sides, seam, sem1, sem2, sem3, sem4, sem5,
    ups2, sides2, seam2, *sems2,
):
    g = lax.axis_index("face")
    b = lax.axis_index("rows")
    pairs = (
        (innov_hbm, innov), (dest_hbm, dest), (cells_hbm, cells), (tiles_hbm, tiles),
        (a_hbm, a), (cy_hbm, cy), (cx_hbm, cx),
    )
    loads = [pltpu.make_async_copy(src, dst, load_sem.at[i]) for i, (src, dst) in enumerate(pairs)]
    for load in loads:
        load.start()
    halo = Halo(ups, sides, seam, below, side_in, rot, (sem1, sem2, sem3, sem4, sem5))
    halo2 = Halo(ups2, sides2, seam2, below2, side_in2, rot2, sems2)
    barrier = pltpu.get_barrier_semaphore()
    expected = halo.greet(barrier) + BANDS - 1

    def hello(i, carry):
        pl.semaphore_signal(barrier, inc=1, device_id=(g, (b + i) & (BANDS - 1)), device_id_type=MESH)
        return carry

    lax.fori_loop(1, BANDS, hello, 0)
    halo.zero()
    halo2.zero()
    for load in loads[:4]:
        load.wait()
    pack(tiles, innov, dest, cells, send)
    own = pltpu.make_async_copy(send.at[0, pl.ds(0, SENT)], recv.at[0, pl.ds(0, SENT)], own_sem)
    own.start()

    def packets(which, half, band):
        return pltpu.make_async_remote_copy(
            src_ref=send.at[which, pl.ds(0, SENT)],
            dst_ref=recv.at[which, pl.ds(0, SENT)],
            send_sem=pack_send,
            recv_sem=pack_recv.at[half],
            device_id=(g, band),
            device_id_type=MESH,
        )

    for load in loads[4:]:
        load.wait()

    def lift(l, carry):
        ups[l] = cy[l, :, 0:8, :] * a[l, :, 0:8, :]
        return carry

    lax.fori_loop(0, LEV, lift, 0)
    west(cx[:, 0, :, 0:LANES] * a[:, 0, :, 0:LANES], sides)
    pl.semaphore_wait(barrier, expected)
    halo.start_rotated()
    halo.side().start()
    for half in range(2):

        def ship(i, carry, half=half):
            packets(i, half, (b + i) & (BANDS - 1)).start()
            return carry

        lax.fori_loop(max(1, half * HALF), (half + 1) * HALF, ship, 0)
    halo.start_rows()
    halo.relay()
    interior(a, cx, cy, out, 0, LEV)
    own.wait()
    edge_row = jnp.zeros((2 * LF * LEV, NC), F32)
    edge_column = jnp.zeros((RD, LEV), F32)
    for half in range(2):
        low = max(1, half * HALF)
        packets(pl.ds(low, (half + 1) * HALF - low), half, b).wait_recv()
        factors(recv, half * HALF, right, top, spot, plain)
        edge_row += dot(top[...], right[...])
        edge_column += dot_t(spot[...], plain[0:LEV]) + dot_t(spot[...], plain[LEV:])
    halo.side().wait_recv()
    halo.wait_rotated()
    patch_rotated(out, rot, 0, LEV)
    patch_west(out, side_in, 0, LEV)
    edge_row = edge_row[: LF * LEV] + edge_row[LF * LEV :]
    for l in range(LEV):
        for f in range(LF):
            value = out[l, f, 0:1, :] + edge_row[f * LEV + l : f * LEV + l + 1]
            ups2[l, f, 0:1, :] = cy[l, f, 0:1, :] * value
    halo2.start_rotated()
    halo.wait_rows()
    patch_rows(out, below, 0, LEV)
    edge_column = jnp.concatenate([edge_column, jnp.zeros((RD, LANES - LEV), F32)], axis=1)
    west(out[:, 0, :, 0:LANES], sides2)
    west(cx[:, 0, :, 0:LANES], sides_x)
    sides2[...] = (sides2[...] + edge_column) * sides_x[...]
    halo2.side().start()
    halo2.start_rows()
    widen_rows(recv, values, index)
    halo2.relay()
    halo2.wait_rows()
    halo2.side().wait_recv()
    halo2.wait_rotated()
    halo.finish()
    halo2.finish()
    packets(pl.ds(1, BANDS - 1), 0, b).wait_send()


def widen_rows(recv, values, index):
    shift = lax.shift_right_logical
    from_lane, to_lane = iota((2 * LANES, 8 * LANES), 0) & (LANES - 1), iota((2 * LANES, 8 * LANES), 1)
    widen = (shift(from_lane, 4) == shift(to_lane, 7)) & (
        (from_lane & (LEV - 1)) == shift(to_lane & (LANES - 1), 3)
    )
    widen = jnp.where(widen, 1.0, 0.0).astype(BF16)
    high, mid, _ = split(recv[:, 0 : CAP * 4, :].reshape(BANDS * CAP * 4, LANES))
    wide = dot(jnp.concatenate([high, mid], axis=1), widen)
    values[...] = wide.reshape(BANDS, CAP * 4, 8 * LANES)
    flat = recv.reshape(BANDS * PACK, LANES)
    cell = flat[pl.ds(SENT - 1, BANDS, stride=PACK), :].astype(I32)
    index[...] = (shift(cell, 13) * NC + (cell & (NC - 1))) * 8 + (shift(cell, 10) & 7)


PARTS = 4


def last_kernel(
    values, index, dense, cx, cy, below, side_in, rot, out_hbm, index_s, mid, out, index_sem, sems, *fields
):
    to_scalar = pltpu.make_async_copy(index, index_s, index_sem)
    to_scalar.start()

    def clear(i, carry):
        for field in fields:
            field[pl.ds(i * LANES, LANES), :] = jnp.zeros((LANES, LANES), F32)
        return carry

    lax.fori_loop(0, LF * 2 * NC // LANES, clear, 0)
    to_scalar.wait()
    shift = lax.shift_right_logical
    lane = iota((1, LANES), 1) & 7

    def add(i, carry):
        for e in range(CAP * K):
            code = index_s[i, e]
            line = values[i, e // 8 : e // 8 + 1, e % 8 * LANES : (e % 8 + 1) * LANES]
            field = fields[e % COPIES]
            field[pl.ds(shift(code, 3), 1), :] += jnp.where(lane == (code & 7), line, 0.0)
        return carry

    lax.fori_loop(0, BANDS, add, 0)

    def turn(f, carry):
        for half in range(2):
            for c in range(NC // LANES):
                rows = pl.ds((f * 2 + half) * NC + c * LANES, LANES)
                block = sum(field[rows, :] for field in fields)
                turned = block.T.reshape(LEV, 8, LANES)
                cols = slice(c * LANES, (c + 1) * LANES)
                mid[:, f, half * 8 : half * 8 + 8, cols] = dense[:, f, half * 8 : half * 8 + 8, cols] + turned
        return carry

    lax.fori_loop(0, LF, turn, 0)
    step = LEV // PARTS
    copies = []
    for p in range(PARTS):
        lo, hi = p * step, (p + 1) * step
        interior(mid, cx, cy, out, lo, hi)
        patch_rows(out, below, lo, hi)
        patch_west(out, side_in, lo, hi)
        patch_rotated(out, rot, lo, hi)
        copies.append(pltpu.make_async_copy(out.at[lo:hi], out_hbm.at[lo:hi], sems.at[p]))
        copies[-1].start()
    for copy in copies:
        copy.wait()


def params(mib, cid=None):
    kw = {} if cid is None else dict(collective_id=cid, has_side_effects=True)
    return pltpu.CompilerParams(vmem_limit_bytes=mib * 1024 * 1024, **kw)


def per_device(final_adjoint, courant_x, courant_y, ray_tiles, ray_innov, ray_dest, ray_cols):
    vmem, anywhere = pl.BlockSpec(memory_space=pltpu.VMEM), pl.BlockSpec(memory_space=pl.ANY)
    field = jax.ShapeDtypeStruct(FIELD, F32)
    dma = pltpu.SemaphoreType.DMA
    dense, held_x, held_y, values, index, below, side_in, rot = pl.pallas_call(
        first_kernel,
        out_shape=[field] * 3 + [
            jax.ShapeDtypeStruct((BANDS, CAP * 4, 8 * LANES), F32),
            jax.ShapeDtypeStruct((BANDS, LANES), I32),
        ] + [jax.ShapeDtypeStruct(shape, F32) for shape in landing()],
        in_specs=[anywhere] * 7,
        out_specs=[vmem] * 8,
        scratch_shapes=[
            pltpu.VMEM(FIELD, F32),
            pltpu.VMEM((1, BANDS, RAYS, LEV * K), BF16),
            pltpu.VMEM((1, RAYS, BANDS), BF16),
            pltpu.VMEM((1, 1, BANDS), I32),
            pltpu.VMEM((1, K, BANDS), I32),
            pltpu.VMEM((BANDS, PACK, LANES), F32),
            pltpu.VMEM((BANDS, PACK, LANES), F32),
            pltpu.VMEM((DEPTH, NC), BF16),
            pltpu.VMEM((2 * LF * LEV, DEPTH), BF16),
            pltpu.VMEM((RD, DEPTH), BF16),
            pltpu.VMEM((2 * LEV, DEPTH), BF16),
            pltpu.VMEM(SIDES, F32),
            dma((7,)), dma, dma((2,)), dma,
        ] + [pltpu.VMEM(shape, F32) for shape in landing()] + halo_scratch() + halo_scratch(),
        compiler_params=params(28, 0),
        name="sums_and_edges",
    )(*(
        pltpu.with_memory_space_constraint(value, pltpu.HBM)
        for value in (
            final_adjoint, courant_x, courant_y, ray_tiles,
            jnp.swapaxes(ray_innov, 1, 2), jnp.swapaxes(ray_dest, 1, 2), jnp.swapaxes(ray_cols, 1, 2),
        )
    ))
    return pl.pallas_call(
        last_kernel,
        out_shape=field,
        in_specs=[vmem] * 8,
        out_specs=anywhere,
        scratch_shapes=[
            pltpu.SMEM((BANDS, LANES), I32),
            pltpu.VMEM(FIELD, F32),
            pltpu.VMEM(FIELD, F32),
            dma, dma((PARTS,)),
        ] + [pltpu.VMEM((LF * 2 * NC, LANES), F32)] * COPIES,
        compiler_params=params(28),
        name="forcing_and_step",
    )(values, index, dense, held_x, held_y, below, side_in, rot)


def solution(mesh):
    placed = (
        P(None, "face", "rows", None),
        P(None, "face", "rows", None),
        P(None, "face", "rows", None),
        P("face", "rows", None, None),
        P("face", "rows", None),
        P("face", "rows", None),
        P("face", "rows", None),
    )
    return jax.shard_map(
        per_device,
        mesh=mesh,
        in_specs=placed,
        out_specs=P(None, "face", "rows", None),
        check_vma=False,
    )
```

```python
import functools

import jax
import jax.numpy as jnp
from jax import lax
from jax.experimental import pallas as pl
from jax.experimental.pallas import tpu as pltpu
from jax.sharding import PartitionSpec as P

LEV, LF, RD, NC = 16, 3, 16, 1024
BANDS, RAYS, K, CAP = 64, 16, 32, 2
GROUP = 8
RELAYS = BANDS // GROUP
LANES = 128
PACK = 16
SENT = 9
F32, BF16, I32 = jnp.float32, jnp.bfloat16, jnp.int32
MESH = pl.DeviceIdType.MESH


def iota(shape, dim):
    return lax.broadcasted_iota(I32, shape, dim)


def dot(a, b):
    return jnp.dot(a, b, preferred_element_type=F32)


def dot_t(a, b):
    return lax.dot_general(a, b, (((1,), (1,)), ((), ())), preferred_element_type=F32)


def split(value):
    high = value.astype(BF16)
    rest = value - high.astype(F32)
    mid = rest.astype(BF16)
    return high, mid, rest - mid.astype(F32)


class Halo:
    def __init__(self, ups, sides, seam, below, side_in, rot, sems):
        self.ups, self.sides, self.seam, self.below, self.side_in, self.rot = ups, sides, seam, below, side_in, rot
        self.send, self.recv, self.rot_send, self.fwd_send, self.rot_recv = sems
        self.g = lax.axis_index("face")
        self.b = lax.axis_index("rows")

    def greet(self, barrier):
        g, b = self.g, self.b

        def hello(face, band):
            pl.semaphore_signal(barrier, inc=1, device_id=(face, band), device_id_type=MESH)

        hello(1 - g, b)

        @pl.when(b < BANDS - 1)
        def _():
            hello(g, b + 1)

        @pl.when(b == BANDS - 1)
        def _():
            hello(g, 0)

        @pl.when((b == BANDS - 1) & (g == 0))
        def _():
            hello(1, 0)

        @pl.when((b & (GROUP - 1)) != 0)
        def _():
            hello(g, b & -GROUP)

        @pl.when((b & (GROUP - 1)) == 0)
        def _():
            hello(1 - g, 0)

        @pl.when(((b & (GROUP - 1)) == 0) & (g == 0) & (b != 0))
        def _():
            hello(0, 0)

        relay = ((b & (GROUP - 1)) == 0).astype(I32)
        origin = (b == 0).astype(I32)
        return 2 + relay * (GROUP - 1) + origin * (RELAYS + jnp.where(g == 0, RELAYS - 1, 1))

    def zero(self):
        g, b = self.g, self.b
        edge = jnp.zeros((LEV, 1, NC), F32)

        @pl.when(b == BANDS - 1)
        def _():
            @pl.when(g == 0)
            def _():
                self.below[:, 1] = edge

            @pl.when(g == 1)
            def _():
                self.below[:, 0] = edge
                self.below[:, 2] = edge

        @pl.when(g == 1)
        def _():
            self.rot[1] = jnp.zeros((LEV, LANES), F32)

    def copy(self, src, dst, send, recv, face, band):
        return pltpu.make_async_remote_copy(
            src_ref=src, dst_ref=dst, send_sem=send, recv_sem=recv,
            device_id=(face, band), device_id_type=MESH,
        )

    def row(self, face):
        return self.copy(self.ups.at[:, :, 0:1, :], self.below, self.send.at[0], self.recv.at[0], self.g, face)

    def one(self, src, dst, face, slot):
        return self.copy(
            self.ups.at[:, src, 0:1, :], self.below.at[:, dst], self.send.at[slot], self.recv.at[slot], face, BANDS - 1
        )

    def side(self):
        return self.copy(self.sides, self.side_in, self.send.at[1], self.recv.at[1], 1 - self.g, self.b)

    def piece(self, which, face, r, n):
        lanes = pl.ds(LANES * (RELAYS - 1 - r), LANES)
        return self.copy(
            self.seam.at[which, :, lanes], self.rot.at[which],
            self.rot_send.at[which, r], self.rot_recv.at[which], face, n,
        )

    def start_rotated(self):
        g, b = self.g, self.b

        @pl.when(b == 0)
        def _():
            @pl.when(g == 0)
            def _():
                for l in range(LEV):
                    self.seam[0, l : l + 1, :] = self.ups[l, 2, 0:1, :]
                    self.seam[1, l : l + 1, :] = self.ups[l, 0, 0:1, :]
                for r in range(RELAYS):
                    self.piece(0, 1, r, r * GROUP).start()
                for r in range(1, RELAYS):
                    self.piece(1, 0, r, r * GROUP).start()
                self.rot[1] = self.seam[1, :, NC - LANES :]

            @pl.when(g == 1)
            def _():
                for l in range(LEV):
                    self.seam[0, l : l + 1, :] = self.ups[l, 1, 0:1, :]
                for r in range(RELAYS):
                    self.piece(0, 0, r, r * GROUP).start()

    def start_rows(self):
        g, b = self.g, self.b

        @pl.when(b == 0)
        def _():
            @pl.when(g == 0)
            def _():
                self.one(1, 2, 0, 0).start()

            @pl.when(g == 1)
            def _():
                self.one(0, 1, 1, 0).start()
                self.one(2, 0, 0, 2).start()

        @pl.when(b != 0)
        def _():
            self.row(b - 1).start()

    def forward(self, dst, i):
        return self.copy(
            self.rot.at[dst], self.rot.at[dst], self.fwd_send.at[dst, i], self.rot_recv.at[dst],
            self.g, (self.b & -GROUP) + i,
        )

    def relay(self):
        g, b = self.g, self.b

        @pl.when((b & (GROUP - 1)) == 0)
        def _():
            self.forward(0, 1).wait_recv()
            for i in range(1, GROUP):
                self.forward(0, i).start()

            @pl.when(g == 0)
            def _():
                @pl.when(b != 0)
                def _():
                    self.forward(1, 1).wait_recv()

                for i in range(1, GROUP):
                    self.forward(1, i).start()

    def wait_rotated(self):
        g, b = self.g, self.b

        @pl.when((b & (GROUP - 1)) != 0)
        def _():
            self.forward(0, 1).wait_recv()

            @pl.when(g == 0)
            def _():
                self.forward(1, 1).wait_recv()

    def wait_rows(self):
        g, b = self.g, self.b

        @pl.when(b != BANDS - 1)
        def _():
            self.row(0).wait_recv()

        @pl.when(b == BANDS - 1)
        def _():
            @pl.when(g == 0)
            def _():
                self.one(1, 2, 0, 0).wait_recv()
                self.one(2, 0, 0, 2).wait_recv()

            @pl.when(g == 1)
            def _():
                self.one(0, 1, 1, 0).wait_recv()

    def finish(self):
        g, b = self.g, self.b
        self.side().wait_send()

        @pl.when(b != 0)
        def _():
            self.row(0).wait_send()

        @pl.when(b == 0)
        def _():
            @pl.when(g == 0)
            def _():
                for r in range(RELAYS):
                    self.piece(0, 1, r, r * GROUP).wait_send()
                for r in range(1, RELAYS):
                    self.piece(1, 0, r, r * GROUP).wait_send()
                self.one(1, 2, 0, 0).wait_send()

            @pl.when(g == 1)
            def _():
                for r in range(RELAYS):
                    self.piece(0, 0, r, r * GROUP).wait_send()
                self.one(0, 1, 1, 0).wait_send()
                self.one(2, 0, 0, 2).wait_send()

        @pl.when((b & (GROUP - 1)) == 0)
        def _():
            for i in range(1, GROUP):
                self.forward(0, i).wait_send()

            @pl.when(g == 0)
            def _():
                for i in range(1, GROUP):
                    self.forward(1, i).wait_send()


def landing():
    return [
        (LEV, LF, 1, NC),
        (RD, LANES),
        (2, LEV, LANES),
    ]


def halo_scratch():
    return [
        pltpu.VMEM(UPS, F32),
        pltpu.VMEM(SIDES, F32),
        pltpu.VMEM((2, LEV, NC), F32),
        pltpu.SemaphoreType.DMA((3,)),
        pltpu.SemaphoreType.DMA((3,)),
        pltpu.SemaphoreType.DMA((2, RELAYS)),
        pltpu.SemaphoreType.DMA((2, GROUP)),
        pltpu.SemaphoreType.DMA((2,)),
    ]


UPS = (LEV, LF, 8, NC)
SIDES = (RD, LANES)
FIELD = (LEV, LF, RD, NC)


def west(along, sides):
    lane = iota(SIDES, 1)
    total = jnp.zeros(SIDES, F32)
    for l in range(LEV):
        total = jnp.where(lane == l, jnp.broadcast_to(along[l, :, 0:1], SIDES), total)
    sides[...] = total


def interior(a, cx, cy, out, lo, hi):
    row = iota((RD, NC), 0)
    col = iota((RD, NC), 1)

    def body(l, carry):
        base, rolled = [], []
        for f in range(LF):
            value, x, y = a[l, f], cx[l, f], cy[l, f]
            along, upward = x * value, y * value
            rolled.append(pltpu.roll(along, NC - 1, 1))
            lifted = jnp.where(row < RD - 1, pltpu.roll(upward, RD - 1, 0), 0.0)
            base.append((1.0 - x - y) * value + lifted)
        for f in range(LF):
            beyond = rolled[f + 1] if f + 1 < LF else 0.0
            out[l, f] = base[f] + jnp.where(col < NC - 1, rolled[f], beyond)
        return carry

    lax.fori_loop(lo, hi, body, 0)


def patch_rows(out, below, lo, hi):
    def body(l, carry):
        for f in range(LF):
            out[l, f, RD - 1 : RD, :] += below[l, f]
        return carry

    lax.fori_loop(lo, hi, body, 0)


def patch_west(out, side_in, lo, hi):
    full = (hi - lo, RD, LANES)
    lane = iota(full, 2)
    mine = jnp.where(lane == iota(full, 0) + lo, jnp.broadcast_to(side_in[...][None], full), 0.0)
    right = jnp.sum(mine, axis=2, keepdims=True)
    out[lo:hi, 2, :, NC - LANES :] += jnp.where(lane == LANES - 1, right, 0.0)


def patch_rotated(out, rot, lo, hi):
    g = lax.axis_index("face")
    b = lax.axis_index("rows")
    full = (hi - lo, RD, LANES)
    lane = iota(full, 2)
    place = LANES - 1 - RD * (b & (GROUP - 1)) - iota(full, 1)

    def column(which):
        piece = rot[which, lo:hi, :]
        picked = jnp.where(lane == place, jnp.broadcast_to(piece[:, None, :], full), 0.0)
        return jnp.where(lane == 0, jnp.sum(picked, axis=2, keepdims=True), 0.0)

    out[lo:hi, pl.ds(g, 1), :, 0:LANES] += column(0).reshape(hi - lo, 1, RD, LANES)

    @pl.when(g == 0)
    def _():
        out[lo:hi, 2, :, 0:LANES] += column(1)


def pack(tiles, innov, dest, cells, send):
    blocks = BANDS
    wide = blocks * RAYS
    ray = iota((RAYS, wide), 1) & (RAYS - 1)
    repeat = (lax.shift_right_logical(iota((blocks, wide), 1), 4) == iota((blocks, wide), 0)).astype(BF16)
    lines = jnp.where(ray == iota((RAYS, wide), 0), dot(innov[0], repeat), 0.0)
    weight = jnp.sum(lines, axis=0, keepdims=True)

    square = (blocks, blocks)
    first, second = iota(square, 0), iota(square, 1)
    target = jnp.broadcast_to(dest[0].astype(F32), square)
    other = dot(jnp.where(first == second, target, 0.0).astype(BF16), jnp.ones(square, BF16))
    same = (other == target) & (first < second)
    order = jnp.sum(same.astype(F32), axis=0, keepdims=True)
    slot = iota((CAP * BANDS, blocks), 0)
    band = ((slot + lax.axis_index("rows")) & (BANDS - 1)).astype(F32)
    turn = lax.shift_right_logical(slot, 6).astype(F32)
    chosen = ((band == target[0:1]) & (turn == order)).astype(BF16)

    sums = dot((dot(chosen, repeat) * weight).astype(BF16), tiles[0].reshape(wide, LEV * K))
    src, dst = iota((LEV * K, LEV * K), 0), iota((LEV * K, LEV * K), 1)
    inner = lax.shift_right_logical(dst & (LANES - 1), 4)
    part = lax.shift_right_logical(dst, 7)
    mixed = (src == (dst & (LEV - 1)) * K + part * 8 + inner).astype(BF16)
    high, mid, low = split(sums)
    sums = dot(high, mixed) + dot(mid, mixed) + dot(low.astype(BF16), mixed)

    cell = cells[0]
    upper = lax.shift_right_logical(cell, 8).astype(F32).astype(BF16)
    lower = (cell & 255).astype(F32).astype(BF16)
    codes = dot_t(chosen, upper) * 256.0 + dot_t(chosen, lower)
    codes = jnp.concatenate(
        [codes[:BANDS], codes[BANDS:], jnp.zeros((BANDS, LANES - 2 * K), F32)], axis=1
    )
    flat = send.reshape(BANDS * PACK, LANES)
    for s in range(CAP):
        for q in range(4):
            flat[pl.ds(s * 4 + q, BANDS, stride=PACK), :] = sums[
                s * BANDS : (s + 1) * BANDS, q * LANES : (q + 1) * LANES
            ]
    flat[pl.ds(SENT - 1, BANDS, stride=PACK), :] = codes


HALF = BANDS // 2
DEPTH = HALF * CAP * K
COPIES = 6


def factors(recv, first, right, top, spot, plain):
    flat = recv.reshape(BANDS * PACK, LANES)
    at = first * PACK
    codes = flat[pl.ds(at + SENT - 1, HALF, stride=PACK), :]
    column = iota((LANES, NC), 1)
    spot_row = iota((RD, LANES), 0)
    for pair in range(2):
        spots = [(s, 2 * pair + half) for half in range(2) for s in range(CAP)]
        sums = jnp.concatenate(
            [flat[pl.ds(at + s * 4 + q, HALF, stride=PACK), :] for s, q in spots], axis=0
        ).T
        cells = jnp.concatenate(
            [pltpu.roll(codes, (LANES - s * K - q * 8) % LANES, 1) for s, q in spots], axis=0
        )
        turned = cells.T.astype(I32)
        rows = lax.shift_right_logical(turned, 10)
        edge = jnp.where((turned & (NC - 1)) == 0, rows, LF * RD)
        cols = cells.astype(I32) & (NC - 1)
        for inner in range(8):
            part = slice((pair * 8 + inner) * LANES, (pair * 8 + inner + 1) * LANES)
            high, mid, _ = split(sums[inner * LEV : (inner + 1) * LEV])
            row = rows[inner : inner + 1]
            for n, term in enumerate((high, mid)):
                plain[n * LEV : (n + 1) * LEV, part] = term
                for f in range(LF):
                    kept = jnp.where(row == f * RD, term.astype(F32), 0.0).astype(BF16)
                    top[(n * LF + f) * LEV : (n * LF + f + 1) * LEV, part] = kept
            spot[:, part] = jnp.where(spot_row == edge[inner : inner + 1], 1.0, 0.0).astype(BF16)
            right[part, :] = jnp.where(column == cols[:, inner : inner + 1], 1.0, 0.0).astype(BF16)


def first_kernel(
    a_hbm, cx_hbm, cy_hbm, tiles_hbm, innov_hbm, dest_hbm, cells_hbm,
    out, cx, cy, values, index, below2, side_in2, rot2,
    a, tiles, innov, dest, cells, send, recv, right, top, spot, plain, sides_x, load_sem, pack_send, pack_recv, own_sem,
    below, side_in, rot, ups, sides, seam, sem1, sem2, sem3, sem4, sem5,
    ups2, sides2, seam2, *sems2,
):
    g = lax.axis_index("face")
    b = lax.axis_index("rows")
    pairs = (
        (innov_hbm, innov), (dest_hbm, dest), (cells_hbm, cells), (tiles_hbm, tiles),
        (a_hbm, a), (cy_hbm, cy), (cx_hbm, cx),
    )
    loads = [pltpu.make_async_copy(src, dst, load_sem.at[i]) for i, (src, dst) in enumerate(pairs)]
    for load in loads:
        load.start()
    halo = Halo(ups, sides, seam, below, side_in, rot, (sem1, sem2, sem3, sem4, sem5))
    halo2 = Halo(ups2, sides2, seam2, below2, side_in2, rot2, sems2)
    barrier = pltpu.get_barrier_semaphore()
    expected = halo.greet(barrier) + BANDS - 1

    def hello(i, carry):
        pl.semaphore_signal(barrier, inc=1, device_id=(g, (b + i) & (BANDS - 1)), device_id_type=MESH)
        return carry

    lax.fori_loop(1, BANDS, hello, 0)
    halo.zero()
    halo2.zero()
    for load in loads[:4]:
        load.wait()
    pack(tiles, innov, dest, cells, send)
    own = pltpu.make_async_copy(send.at[0, pl.ds(0, SENT)], recv.at[0, pl.ds(0, SENT)], own_sem)
    own.start()

    def packets(which, half, band):
        return pltpu.make_async_remote_copy(
            src_ref=send.at[which, pl.ds(0, SENT)],
            dst_ref=recv.at[which, pl.ds(0, SENT)],
            send_sem=pack_send,
            recv_sem=pack_recv.at[half],
            device_id=(g, band),
            device_id_type=MESH,
        )

    for load in loads[4:]:
        load.wait()

    def lift(l, carry):
        ups[l] = cy[l, :, 0:8, :] * a[l, :, 0:8, :]
        return carry

    lax.fori_loop(0, LEV, lift, 0)
    west(cx[:, 0, :, 0:LANES] * a[:, 0, :, 0:LANES], sides)
    pl.semaphore_wait(barrier, expected)
    halo.start_rotated()
    halo.side().start()
    for half in range(2):

        def ship(i, carry, half=half):
            packets(i, half, (b + i) & (BANDS - 1)).start()
            return carry

        lax.fori_loop(max(1, half * HALF), (half + 1) * HALF, ship, 0)
    halo.start_rows()
    halo.relay()
    interior(a, cx, cy, out, 0, LEV)
    own.wait()
    edge_row = jnp.zeros((2 * LF * LEV, NC), F32)
    edge_column = jnp.zeros((RD, LEV), F32)
    for half in range(2):
        low = max(1, half * HALF)
        packets(pl.ds(low, (half + 1) * HALF - low), half, b).wait_recv()
        factors(recv, half * HALF, right, top, spot, plain)
        edge_row += dot(top[...], right[...])
        edge_column += dot_t(spot[...], plain[0:LEV]) + dot_t(spot[...], plain[LEV:])
    halo.side().wait_recv()
    halo.wait_rotated()
    patch_rotated(out, rot, 0, LEV)
    patch_west(out, side_in, 0, LEV)
    edge_row = edge_row[: LF * LEV] + edge_row[LF * LEV :]
    for l in range(LEV):
        for f in range(LF):
            value = out[l, f, 0:1, :] + edge_row[f * LEV + l : f * LEV + l + 1]
            ups2[l, f, 0:1, :] = cy[l, f, 0:1, :] * value
    halo2.start_rotated()
    halo.wait_rows()
    patch_rows(out, below, 0, LEV)
    edge_column = jnp.concatenate([edge_column, jnp.zeros((RD, LANES - LEV), F32)], axis=1)
    west(out[:, 0, :, 0:LANES], sides2)
    west(cx[:, 0, :, 0:LANES], sides_x)
    sides2[...] = (sides2[...] + edge_column) * sides_x[...]
    halo2.side().start()
    halo2.start_rows()
    widen_rows(recv, values, index)
    halo2.relay()
    halo2.wait_rows()
    halo2.side().wait_recv()
    halo2.wait_rotated()
    halo.finish()
    halo2.finish()
    packets(pl.ds(1, BANDS - 1), 0, b).wait_send()


def widen_rows(recv, values, index):
    shift = lax.shift_right_logical
    wide = (2 * LANES, 8 * LANES)
    from_lane, to_lane = iota(wide, 0) & (LANES - 1), iota(wide, 1)
    block, inner = shift(to_lane, 7), to_lane & (LANES - 1)
    widen = (shift(from_lane, 4) == block) & ((from_lane & (LEV - 1)) == shift(inner, 3))
    widen = jnp.where(widen, 1.0, 0.0).astype(BF16)
    flat = recv.reshape(BANDS * PACK, LANES)
    cell = flat[pl.ds(SENT - 1, BANDS, stride=PACK), :].astype(I32)
    index[...] = shift(cell, 13) * NC + (cell & (NC - 1))
    lower = (shift(cell, 10) & 7).astype(F32).astype(BF16)
    own = (iota((BANDS, 8 * LANES), 1) & 7).astype(F32)
    for s in range(CAP * 4):
        high, mid, _ = split(flat[pl.ds(s, BANDS, stride=PACK), :])
        lines = dot(jnp.concatenate([high, mid], axis=1), widen)
        spread = jnp.where(from_lane[:LANES] == s * 8 + block[:LANES], 1.0, 0.0).astype(BF16)
        lines = jnp.where(dot(lower, spread) == own, lines, 0.0)
        for p in range(8):
            values[s * 8 + p] = lines[:, p * LANES : (p + 1) * LANES]


PARTS = 4


def last_kernel(
    values, index, dense, cx, cy, below, side_in, rot, out_hbm, index_s, mid, out, index_sem, sems, *fields
):
    to_scalar = pltpu.make_async_copy(index, index_s, index_sem)
    to_scalar.start()

    def clear(i, carry):
        for field in fields:
            field[pl.ds(i * LANES, LANES), :] = jnp.zeros((LANES, LANES), F32)
        return carry

    lax.fori_loop(0, LF * 2 * NC // LANES, clear, 0)
    to_scalar.wait()
    def add(i, carry):
        for e in range(BANDS):
            field = fields[e % COPIES]
            field[pl.ds(index_s[e, i], 1), :] += values[i, e : e + 1, :]
        return carry

    lax.fori_loop(0, CAP * K, add, 0)

    def turn(f, carry):
        for half in range(2):
            for c in range(NC // LANES):
                rows = pl.ds((f * 2 + half) * NC + c * LANES, LANES)
                block = sum(field[rows, :] for field in fields)
                turned = block.T.reshape(LEV, 8, LANES)
                cols = slice(c * LANES, (c + 1) * LANES)
                mid[:, f, half * 8 : half * 8 + 8, cols] = dense[:, f, half * 8 : half * 8 + 8, cols] + turned
        return carry

    lax.fori_loop(0, LF, turn, 0)
    step = LEV // PARTS
    copies = []
    for p in range(PARTS):
        lo, hi = p * step, (p + 1) * step
        interior(mid, cx, cy, out, lo, hi)
        patch_rows(out, below, lo, hi)
        patch_west(out, side_in, lo, hi)
        patch_rotated(out, rot, lo, hi)
        copies.append(pltpu.make_async_copy(out.at[lo:hi], out_hbm.at[lo:hi], sems.at[p]))
        copies[-1].start()
    for copy in copies:
        copy.wait()


def params(mib, cid=None):
    kw = {} if cid is None else dict(collective_id=cid, has_side_effects=True)
    return pltpu.CompilerParams(vmem_limit_bytes=mib * 1024 * 1024, **kw)


def per_device(final_adjoint, courant_x, courant_y, ray_tiles, ray_innov, ray_dest, ray_cols):
    vmem, anywhere = pl.BlockSpec(memory_space=pltpu.VMEM), pl.BlockSpec(memory_space=pl.ANY)
    field = jax.ShapeDtypeStruct(FIELD, F32)
    dma = pltpu.SemaphoreType.DMA
    dense, held_x, held_y, values, index, below, side_in, rot = pl.pallas_call(
        first_kernel,
        out_shape=[field] * 3 + [
            jax.ShapeDtypeStruct((CAP * K, BANDS, LANES), F32),
            jax.ShapeDtypeStruct((BANDS, LANES), I32),
        ] + [jax.ShapeDtypeStruct(shape, F32) for shape in landing()],
        in_specs=[anywhere] * 7,
        out_specs=[vmem] * 8,
        scratch_shapes=[
            pltpu.VMEM(FIELD, F32),
            pltpu.VMEM((1, BANDS, RAYS, LEV * K), BF16),
            pltpu.VMEM((1, RAYS, BANDS), BF16),
            pltpu.VMEM((1, 1, BANDS), I32),
            pltpu.VMEM((1, K, BANDS), I32),
            pltpu.VMEM((BANDS, PACK, LANES), F32),
            pltpu.VMEM((BANDS, PACK, LANES), F32),
            pltpu.VMEM((DEPTH, NC), BF16),
            pltpu.VMEM((2 * LF * LEV, DEPTH), BF16),
            pltpu.VMEM((RD, DEPTH), BF16),
            pltpu.VMEM((2 * LEV, DEPTH), BF16),
            pltpu.VMEM(SIDES, F32),
            dma((7,)), dma, dma((2,)), dma,
        ] + [pltpu.VMEM(shape, F32) for shape in landing()] + halo_scratch() + halo_scratch(),
        compiler_params=params(28, 0),
        name="sums_and_edges",
    )(*(
        pltpu.with_memory_space_constraint(value, pltpu.HBM)
        for value in (
            final_adjoint, courant_x, courant_y, ray_tiles,
            jnp.swapaxes(ray_innov, 1, 2), jnp.swapaxes(ray_dest, 1, 2), jnp.swapaxes(ray_cols, 1, 2),
        )
    ))
    return pl.pallas_call(
        last_kernel,
        out_shape=field,
        in_specs=[vmem] * 8,
        out_specs=anywhere,
        scratch_shapes=[
            pltpu.SMEM((BANDS, LANES), I32),
            pltpu.VMEM(FIELD, F32),
            pltpu.VMEM(FIELD, F32),
            dma, dma((PARTS,)),
        ] + [pltpu.VMEM((LF * 2 * NC, LANES), F32)] * COPIES,
        compiler_params=params(34),
        name="forcing_and_step",
    )(values, index, dense, held_x, held_y, below, side_in, rot)


def solution(mesh):
    placed = (
        P(None, "face", "rows", None),
        P(None, "face", "rows", None),
        P(None, "face", "rows", None),
        P("face", "rows", None, None),
        P("face", "rows", None),
        P("face", "rows", None),
        P("face", "rows", None),
    )
    return jax.shard_map(
        per_device,
        mesh=mesh,
        in_specs=placed,
        out_specs=P(None, "face", "rows", None),
        check_vma=False,
    )
```

```python
import functools

import jax
import jax.numpy as jnp
from jax import lax
from jax.experimental import pallas as pl
from jax.experimental.pallas import tpu as pltpu
from jax.sharding import PartitionSpec as P

LEV, LF, RD, NC = 16, 3, 16, 1024
BANDS, RAYS, K, CAP = 64, 16, 32, 2
GROUP = 8
RELAYS = BANDS // GROUP
LANES = 128
PACK = 16
SENT = 9
F32, BF16, I32 = jnp.float32, jnp.bfloat16, jnp.int32
MESH = pl.DeviceIdType.MESH


def iota(shape, dim):
    return lax.broadcasted_iota(I32, shape, dim)


def dot(a, b):
    return jnp.dot(a, b, preferred_element_type=F32)


def dot_t(a, b):
    return lax.dot_general(a, b, (((1,), (1,)), ((), ())), preferred_element_type=F32)


def split(value):
    high = value.astype(BF16)
    rest = value - high.astype(F32)
    mid = rest.astype(BF16)
    return high, mid, rest - mid.astype(F32)


class Halo:
    def __init__(self, ups, sides, seam, below, side_in, rot, sems):
        self.ups, self.sides, self.seam, self.below, self.side_in, self.rot = ups, sides, seam, below, side_in, rot
        self.send, self.recv, self.rot_send, self.fwd_send, self.rot_recv = sems
        self.g = lax.axis_index("face")
        self.b = lax.axis_index("rows")

    def greet(self, barrier):
        g, b = self.g, self.b

        def hello(face, band):
            pl.semaphore_signal(barrier, inc=1, device_id=(face, band), device_id_type=MESH)

        hello(1 - g, b)

        @pl.when(b < BANDS - 1)
        def _():
            hello(g, b + 1)

        @pl.when(b == BANDS - 1)
        def _():
            hello(g, 0)

        @pl.when((b == BANDS - 1) & (g == 0))
        def _():
            hello(1, 0)

        @pl.when((b & (GROUP - 1)) != 0)
        def _():
            hello(g, b & -GROUP)

        @pl.when((b & (GROUP - 1)) == 0)
        def _():
            hello(1 - g, 0)

        @pl.when(((b & (GROUP - 1)) == 0) & (g == 0) & (b != 0))
        def _():
            hello(0, 0)

        relay = ((b & (GROUP - 1)) == 0).astype(I32)
        origin = (b == 0).astype(I32)
        return 2 + relay * (GROUP - 1) + origin * (RELAYS + jnp.where(g == 0, RELAYS - 1, 1))

    def zero(self):
        g, b = self.g, self.b
        edge = jnp.zeros((LEV, 1, NC), F32)

        @pl.when(b == BANDS - 1)
        def _():
            @pl.when(g == 0)
            def _():
                self.below[:, 1] = edge

            @pl.when(g == 1)
            def _():
                self.below[:, 0] = edge
                self.below[:, 2] = edge

        @pl.when(g == 1)
        def _():
            self.rot[1] = jnp.zeros((LEV, LANES), F32)

    def copy(self, src, dst, send, recv, face, band):
        return pltpu.make_async_remote_copy(
            src_ref=src, dst_ref=dst, send_sem=send, recv_sem=recv,
            device_id=(face, band), device_id_type=MESH,
        )

    def row(self, face):
        return self.copy(self.ups.at[:, :, 0:1, :], self.below, self.send.at[0], self.recv.at[0], self.g, face)

    def one(self, src, dst, face, slot):
        return self.copy(
            self.ups.at[:, src, 0:1, :], self.below.at[:, dst], self.send.at[slot], self.recv.at[slot], face, BANDS - 1
        )

    def side(self):
        return self.copy(self.sides, self.side_in, self.send.at[1], self.recv.at[1], 1 - self.g, self.b)

    def piece(self, which, face, r, n):
        lanes = pl.ds(LANES * (RELAYS - 1 - r), LANES)
        return self.copy(
            self.seam.at[which, :, lanes], self.rot.at[which],
            self.rot_send.at[which, r], self.rot_recv.at[which], face, n,
        )

    def start_rotated(self):
        g, b = self.g, self.b

        @pl.when(b == 0)
        def _():
            @pl.when(g == 0)
            def _():
                for l in range(LEV):
                    self.seam[0, l : l + 1, :] = self.ups[l, 2, 0:1, :]
                    self.seam[1, l : l + 1, :] = self.ups[l, 0, 0:1, :]
                for r in range(RELAYS):
                    self.piece(0, 1, r, r * GROUP).start()
                for r in range(1, RELAYS):
                    self.piece(1, 0, r, r * GROUP).start()
                self.rot[1] = self.seam[1, :, NC - LANES :]

            @pl.when(g == 1)
            def _():
                for l in range(LEV):
                    self.seam[0, l : l + 1, :] = self.ups[l, 1, 0:1, :]
                for r in range(RELAYS):
                    self.piece(0, 0, r, r * GROUP).start()

    def start_rows(self):
        g, b = self.g, self.b

        @pl.when(b == 0)
        def _():
            @pl.when(g == 0)
            def _():
                self.one(1, 2, 0, 0).start()

            @pl.when(g == 1)
            def _():
                self.one(0, 1, 1, 0).start()
                self.one(2, 0, 0, 2).start()

        @pl.when(b != 0)
        def _():
            self.row(b - 1).start()

    def forward(self, dst, i):
        return self.copy(
            self.rot.at[dst], self.rot.at[dst], self.fwd_send.at[dst, i], self.rot_recv.at[dst],
            self.g, (self.b & -GROUP) + i,
        )

    def relay(self):
        g, b = self.g, self.b

        @pl.when((b & (GROUP - 1)) == 0)
        def _():
            self.forward(0, 1).wait_recv()
            for i in range(1, GROUP):
                self.forward(0, i).start()

            @pl.when(g == 0)
            def _():
                @pl.when(b != 0)
                def _():
                    self.forward(1, 1).wait_recv()

                for i in range(1, GROUP):
                    self.forward(1, i).start()

    def wait_rotated(self):
        g, b = self.g, self.b

        @pl.when((b & (GROUP - 1)) != 0)
        def _():
            self.forward(0, 1).wait_recv()

            @pl.when(g == 0)
            def _():
                self.forward(1, 1).wait_recv()

    def wait_rows(self):
        g, b = self.g, self.b

        @pl.when(b != BANDS - 1)
        def _():
            self.row(0).wait_recv()

        @pl.when(b == BANDS - 1)
        def _():
            @pl.when(g == 0)
            def _():
                self.one(1, 2, 0, 0).wait_recv()
                self.one(2, 0, 0, 2).wait_recv()

            @pl.when(g == 1)
            def _():
                self.one(0, 1, 1, 0).wait_recv()

    def finish(self):
        g, b = self.g, self.b
        self.side().wait_send()

        @pl.when(b != 0)
        def _():
            self.row(0).wait_send()

        @pl.when(b == 0)
        def _():
            @pl.when(g == 0)
            def _():
                for r in range(RELAYS):
                    self.piece(0, 1, r, r * GROUP).wait_send()
                for r in range(1, RELAYS):
                    self.piece(1, 0, r, r * GROUP).wait_send()
                self.one(1, 2, 0, 0).wait_send()

            @pl.when(g == 1)
            def _():
                for r in range(RELAYS):
                    self.piece(0, 0, r, r * GROUP).wait_send()
                self.one(0, 1, 1, 0).wait_send()
                self.one(2, 0, 0, 2).wait_send()

        @pl.when((b & (GROUP - 1)) == 0)
        def _():
            for i in range(1, GROUP):
                self.forward(0, i).wait_send()

            @pl.when(g == 0)
            def _():
                for i in range(1, GROUP):
                    self.forward(1, i).wait_send()


def landing():
    return [
        (LEV, LF, 1, NC),
        (RD, LANES),
        (2, LEV, LANES),
    ]


def halo_scratch():
    return [
        pltpu.VMEM(UPS, F32),
        pltpu.VMEM(SIDES, F32),
        pltpu.VMEM((2, LEV, NC), F32),
        pltpu.SemaphoreType.DMA((3,)),
        pltpu.SemaphoreType.DMA((3,)),
        pltpu.SemaphoreType.DMA((2, RELAYS)),
        pltpu.SemaphoreType.DMA((2, GROUP)),
        pltpu.SemaphoreType.DMA((2,)),
    ]


UPS = (LEV, LF, 8, NC)
SIDES = (RD, LANES)
FIELD = (LEV, LF, RD, NC)


def west(along, sides):
    lane = iota(SIDES, 1)
    total = jnp.zeros(SIDES, F32)
    for l in range(LEV):
        total = jnp.where(lane == l, jnp.broadcast_to(along[l, :, 0:1], SIDES), total)
    sides[...] = total


def interior(a, cx, cy, out, lo, hi):
    row = iota((RD, NC), 0)
    col = iota((RD, NC), 1)

    def body(l, carry):
        base, rolled = [], []
        for f in range(LF):
            value, x, y = a[l, f], cx[l, f], cy[l, f]
            along, upward = x * value, y * value
            rolled.append(pltpu.roll(along, NC - 1, 1))
            lifted = jnp.where(row < RD - 1, pltpu.roll(upward, RD - 1, 0), 0.0)
            base.append((1.0 - x - y) * value + lifted)
        for f in range(LF):
            beyond = rolled[f + 1] if f + 1 < LF else 0.0
            out[l, f] = base[f] + jnp.where(col < NC - 1, rolled[f], beyond)
        return carry

    lax.fori_loop(lo, hi, body, 0)


def patch_rows(out, below, lo, hi):
    def body(l, carry):
        for f in range(LF):
            out[l, f, RD - 1 : RD, :] += below[l, f]
        return carry

    lax.fori_loop(lo, hi, body, 0)


def patch_west(out, side_in, lo, hi):
    full = (hi - lo, RD, LANES)
    lane = iota(full, 2)
    mine = jnp.where(lane == iota(full, 0) + lo, jnp.broadcast_to(side_in[...][None], full), 0.0)
    right = jnp.sum(mine, axis=2, keepdims=True)
    out[lo:hi, 2, :, NC - LANES :] += jnp.where(lane == LANES - 1, right, 0.0)


def patch_rotated(out, rot, lo, hi):
    g = lax.axis_index("face")
    b = lax.axis_index("rows")
    full = (hi - lo, RD, LANES)
    lane = iota(full, 2)
    place = LANES - 1 - RD * (b & (GROUP - 1)) - iota(full, 1)

    def column(which):
        piece = rot[which, lo:hi, :]
        picked = jnp.where(lane == place, jnp.broadcast_to(piece[:, None, :], full), 0.0)
        return jnp.where(lane == 0, jnp.sum(picked, axis=2, keepdims=True), 0.0)

    out[lo:hi, pl.ds(g, 1), :, 0:LANES] += column(0).reshape(hi - lo, 1, RD, LANES)

    @pl.when(g == 0)
    def _():
        out[lo:hi, 2, :, 0:LANES] += column(1)


def pack(tiles, innov, dest, cells, send):
    blocks = BANDS
    wide = blocks * RAYS
    ray = iota((RAYS, wide), 1) & (RAYS - 1)
    repeat = (lax.shift_right_logical(iota((blocks, wide), 1), 4) == iota((blocks, wide), 0)).astype(BF16)
    lines = jnp.where(ray == iota((RAYS, wide), 0), dot(innov[0], repeat), 0.0)
    weight = jnp.sum(lines, axis=0, keepdims=True)

    square = (blocks, blocks)
    first, second = iota(square, 0), iota(square, 1)
    target = jnp.broadcast_to(dest[0].astype(F32), square)
    other = dot(jnp.where(first == second, target, 0.0).astype(BF16), jnp.ones(square, BF16))
    same = (other == target) & (first < second)
    order = jnp.sum(same.astype(F32), axis=0, keepdims=True)
    slot = iota((CAP * BANDS, blocks), 0)
    band = ((slot + lax.axis_index("rows")) & (BANDS - 1)).astype(F32)
    turn = lax.shift_right_logical(slot, 6).astype(F32)
    chosen = ((band == target[0:1]) & (turn == order)).astype(BF16)

    sums = dot((dot(chosen, repeat) * weight).astype(BF16), tiles[0].reshape(wide, LEV * K))
    src, dst = iota((LEV * K, LEV * K), 0), iota((LEV * K, LEV * K), 1)
    inner = lax.shift_right_logical(dst & (LANES - 1), 4)
    part = lax.shift_right_logical(dst, 7)
    mixed = (src == (dst & (LEV - 1)) * K + part * 8 + inner).astype(BF16)
    high, mid, low = split(sums)
    sums = dot(high, mixed) + dot(mid, mixed) + dot(low.astype(BF16), mixed)

    cell = cells[0]
    upper = lax.shift_right_logical(cell, 8).astype(F32).astype(BF16)
    lower = (cell & 255).astype(F32).astype(BF16)
    codes = dot_t(chosen, upper) * 256.0 + dot_t(chosen, lower)
    codes = jnp.concatenate(
        [codes[:BANDS], codes[BANDS:], jnp.zeros((BANDS, LANES - 2 * K), F32)], axis=1
    )
    flat = send.reshape(BANDS * PACK, LANES)
    for s in range(CAP):
        for q in range(4):
            flat[pl.ds(s * 4 + q, BANDS, stride=PACK), :] = sums[
                s * BANDS : (s + 1) * BANDS, q * LANES : (q + 1) * LANES
            ]
    flat[pl.ds(SENT - 1, BANDS, stride=PACK), :] = codes


HALF = BANDS // 2
DEPTH = HALF * CAP * K
COPIES = 6


def factors(recv, first, right, top, spot, plain):
    flat = recv.reshape(BANDS * PACK, LANES)
    at = first * PACK
    codes = flat[pl.ds(at + SENT - 1, HALF, stride=PACK), :]
    column = iota((LANES, NC), 1)
    spot_row = iota((RD, LANES), 0)
    for pair in range(2):
        spots = [(s, 2 * pair + half) for half in range(2) for s in range(CAP)]
        sums = jnp.concatenate(
            [flat[pl.ds(at + s * 4 + q, HALF, stride=PACK), :] for s, q in spots], axis=0
        ).T
        cells = jnp.concatenate(
            [pltpu.roll(codes, (LANES - s * K - q * 8) % LANES, 1) for s, q in spots], axis=0
        )
        turned = cells.T.astype(I32)
        rows = lax.shift_right_logical(turned, 10)
        edge = jnp.where((turned & (NC - 1)) == 0, rows, LF * RD)
        cols = cells.astype(I32) & (NC - 1)
        for inner in range(8):
            part = slice((pair * 8 + inner) * LANES, (pair * 8 + inner + 1) * LANES)
            high, mid, _ = split(sums[inner * LEV : (inner + 1) * LEV])
            row = rows[inner : inner + 1]
            for n, term in enumerate((high, mid)):
                plain[n * LEV : (n + 1) * LEV, part] = term
                for f in range(LF):
                    kept = jnp.where(row == f * RD, term.astype(F32), 0.0).astype(BF16)
                    top[(n * LF + f) * LEV : (n * LF + f + 1) * LEV, part] = kept
            spot[:, part] = jnp.where(spot_row == edge[inner : inner + 1], 1.0, 0.0).astype(BF16)
            right[part, :] = jnp.where(column == cols[:, inner : inner + 1], 1.0, 0.0).astype(BF16)


def first_kernel(
    a_hbm, cx_hbm, cy_hbm, tiles_hbm, innov_hbm, dest_hbm, cells_hbm,
    out, cx, cy, values, index, below2, side_in2, rot2,
    a, tiles, innov, dest, cells, send, recv, right, top, spot, plain, sides_x, load_sem, pack_send, pack_recv, own_sem,
    below, side_in, rot, ups, sides, seam, sem1, sem2, sem3, sem4, sem5,
    ups2, sides2, seam2, *sems2,
):
    g = lax.axis_index("face")
    b = lax.axis_index("rows")
    pairs = (
        (innov_hbm, innov), (dest_hbm, dest), (cells_hbm, cells), (tiles_hbm, tiles),
        (a_hbm, a), (cy_hbm, cy), (cx_hbm, cx),
    )
    loads = [pltpu.make_async_copy(src, dst, load_sem.at[i]) for i, (src, dst) in enumerate(pairs)]
    for load in loads:
        load.start()
    halo = Halo(ups, sides, seam, below, side_in, rot, (sem1, sem2, sem3, sem4, sem5))
    halo2 = Halo(ups2, sides2, seam2, below2, side_in2, rot2, sems2)
    barrier = pltpu.get_barrier_semaphore()
    expected = halo.greet(barrier) + BANDS - 1

    def hello(i, carry):
        pl.semaphore_signal(barrier, inc=1, device_id=(g, (b + i) & (BANDS - 1)), device_id_type=MESH)
        return carry

    lax.fori_loop(1, BANDS, hello, 0)
    halo.zero()
    halo2.zero()
    for load in loads[:4]:
        load.wait()
    pack(tiles, innov, dest, cells, send)
    own = pltpu.make_async_copy(send.at[0, pl.ds(0, SENT)], recv.at[0, pl.ds(0, SENT)], own_sem)
    own.start()

    def packets(which, half, band):
        return pltpu.make_async_remote_copy(
            src_ref=send.at[which, pl.ds(0, SENT)],
            dst_ref=recv.at[which, pl.ds(0, SENT)],
            send_sem=pack_send,
            recv_sem=pack_recv.at[half],
            device_id=(g, band),
            device_id_type=MESH,
        )

    for load in loads[4:]:
        load.wait()

    def lift(l, carry):
        ups[l] = cy[l, :, 0:8, :] * a[l, :, 0:8, :]
        return carry

    lax.fori_loop(0, LEV, lift, 0)
    west(cx[:, 0, :, 0:LANES] * a[:, 0, :, 0:LANES], sides)
    pl.semaphore_wait(barrier, expected)
    halo.start_rotated()
    halo.side().start()
    for half in (1, 0):

        def ship(i, carry, half=half):
            packets(i, half, (b + i) & (BANDS - 1)).start()
            return carry

        lax.fori_loop(max(1, half * HALF), (half + 1) * HALF, ship, 0)
    halo.start_rows()
    halo.relay()
    interior(a, cx, cy, out, 0, LEV)
    own.wait()
    edge_row = jnp.zeros((2 * LF * LEV, NC), F32)
    edge_column = jnp.zeros((RD, LEV), F32)
    for half in (1, 0):
        low = max(1, half * HALF)
        packets(pl.ds(low, (half + 1) * HALF - low), half, b).wait_recv()
        factors(recv, half * HALF, right, top, spot, plain)
        edge_row += dot(top[...], right[...])
        edge_column += dot_t(spot[...], plain[0:LEV]) + dot_t(spot[...], plain[LEV:])
    halo.side().wait_recv()
    halo.wait_rotated()
    patch_rotated(out, rot, 0, LEV)
    patch_west(out, side_in, 0, LEV)
    edge_row = edge_row[: LF * LEV] + edge_row[LF * LEV :]
    for l in range(LEV):
        for f in range(LF):
            value = out[l, f, 0:1, :] + edge_row[f * LEV + l : f * LEV + l + 1]
            ups2[l, f, 0:1, :] = cy[l, f, 0:1, :] * value
    halo2.start_rotated()
    halo.wait_rows()
    patch_rows(out, below, 0, LEV)
    edge_column = jnp.concatenate([edge_column, jnp.zeros((RD, LANES - LEV), F32)], axis=1)
    west(out[:, 0, :, 0:LANES], sides2)
    west(cx[:, 0, :, 0:LANES], sides_x)
    sides2[...] = (sides2[...] + edge_column) * sides_x[...]
    halo2.side().start()
    halo2.start_rows()
    widen_rows(recv, values, index)
    halo2.relay()
    halo2.wait_rows()
    halo2.side().wait_recv()
    halo2.wait_rotated()
    halo.finish()
    halo2.finish()
    packets(pl.ds(1, BANDS - 1), 0, b).wait_send()


def widen_rows(recv, values, index):
    shift = lax.shift_right_logical
    wide = (2 * LANES, 8 * LANES)
    from_lane, to_lane = iota(wide, 0) & (LANES - 1), iota(wide, 1)
    block, inner = shift(to_lane, 7), to_lane & (LANES - 1)
    widen = (shift(from_lane, 4) == block) & ((from_lane & (LEV - 1)) == shift(inner, 3))
    widen = jnp.where(widen, 1.0, 0.0).astype(BF16)
    flat = recv.reshape(BANDS * PACK, LANES)
    cell = flat[pl.ds(SENT - 1, BANDS, stride=PACK), :].astype(I32)
    index[...] = shift(cell, 13) * NC + (cell & (NC - 1))
    lower = (shift(cell, 10) & 7).astype(F32).astype(BF16)
    own = (iota((BANDS, 8 * LANES), 1) & 7).astype(F32)
    for s in range(CAP * 4):
        high, mid, _ = split(flat[pl.ds(s, BANDS, stride=PACK), :])
        lines = dot(jnp.concatenate([high, mid], axis=1), widen)
        spread = jnp.where(from_lane[:LANES] == s * 8 + block[:LANES], 1.0, 0.0).astype(BF16)
        lines = jnp.where(dot(lower, spread) == own, lines, 0.0)
        for p in range(8):
            values[s * 8 + p] = lines[:, p * LANES : (p + 1) * LANES]


PARTS = 4


def last_kernel(
    values, index, dense, cx, cy, below, side_in, rot, out_hbm, index_s, mid, out, index_sem, sems, *fields
):
    to_scalar = pltpu.make_async_copy(index, index_s, index_sem)
    to_scalar.start()

    def clear(i, carry):
        for field in fields:
            field[pl.ds(i * LANES, LANES), :] = jnp.zeros((LANES, LANES), F32)
        return carry

    lax.fori_loop(0, LF * 2 * NC // LANES, clear, 0)
    to_scalar.wait()
    def add(i, carry):
        for e in range(BANDS):
            field = fields[e % COPIES]
            field[pl.ds(index_s[e, i], 1), :] += values[i, e : e + 1, :]
        return carry

    lax.fori_loop(0, CAP * K, add, 0)

    def turn(f, carry):
        for half in range(2):
            for c in range(NC // LANES):
                rows = pl.ds((f * 2 + half) * NC + c * LANES, LANES)
                block = sum(field[rows, :] for field in fields)
                turned = block.T.reshape(LEV, 8, LANES)
                cols = slice(c * LANES, (c + 1) * LANES)
                mid[:, f, half * 8 : half * 8 + 8, cols] = dense[:, f, half * 8 : half * 8 + 8, cols] + turned
        return carry

    lax.fori_loop(0, LF, turn, 0)
    step = LEV // PARTS
    copies = []
    for p in range(PARTS):
        lo, hi = p * step, (p + 1) * step
        interior(mid, cx, cy, out, lo, hi)
        patch_rows(out, below, lo, hi)
        patch_west(out, side_in, lo, hi)
        patch_rotated(out, rot, lo, hi)
        copies.append(pltpu.make_async_copy(out.at[lo:hi], out_hbm.at[lo:hi], sems.at[p]))
        copies[-1].start()
    for copy in copies:
        copy.wait()


def params(mib, cid=None):
    kw = {} if cid is None else dict(collective_id=cid, has_side_effects=True)
    return pltpu.CompilerParams(vmem_limit_bytes=mib * 1024 * 1024, **kw)


def per_device(final_adjoint, courant_x, courant_y, ray_tiles, ray_innov, ray_dest, ray_cols):
    vmem, anywhere = pl.BlockSpec(memory_space=pltpu.VMEM), pl.BlockSpec(memory_space=pl.ANY)
    field = jax.ShapeDtypeStruct(FIELD, F32)
    dma = pltpu.SemaphoreType.DMA
    dense, held_x, held_y, values, index, below, side_in, rot = pl.pallas_call(
        first_kernel,
        out_shape=[field] * 3 + [
            jax.ShapeDtypeStruct((CAP * K, BANDS, LANES), F32),
            jax.ShapeDtypeStruct((BANDS, LANES), I32),
        ] + [jax.ShapeDtypeStruct(shape, F32) for shape in landing()],
        in_specs=[anywhere] * 7,
        out_specs=[vmem] * 8,
        scratch_shapes=[
            pltpu.VMEM(FIELD, F32),
            pltpu.VMEM((1, BANDS, RAYS, LEV * K), BF16),
            pltpu.VMEM((1, RAYS, BANDS), BF16),
            pltpu.VMEM((1, 1, BANDS), I32),
            pltpu.VMEM((1, K, BANDS), I32),
            pltpu.VMEM((BANDS, PACK, LANES), F32),
            pltpu.VMEM((BANDS, PACK, LANES), F32),
            pltpu.VMEM((DEPTH, NC), BF16),
            pltpu.VMEM((2 * LF * LEV, DEPTH), BF16),
            pltpu.VMEM((RD, DEPTH), BF16),
            pltpu.VMEM((2 * LEV, DEPTH), BF16),
            pltpu.VMEM(SIDES, F32),
            dma((7,)), dma, dma((2,)), dma,
        ] + [pltpu.VMEM(shape, F32) for shape in landing()] + halo_scratch() + halo_scratch(),
        compiler_params=params(28, 0),
        name="sums_and_edges",
    )(*(
        pltpu.with_memory_space_constraint(value, pltpu.HBM)
        for value in (
            final_adjoint, courant_x, courant_y, ray_tiles,
            jnp.swapaxes(ray_innov, 1, 2), jnp.swapaxes(ray_dest, 1, 2), jnp.swapaxes(ray_cols, 1, 2),
        )
    ))
    return pl.pallas_call(
        last_kernel,
        out_shape=field,
        in_specs=[vmem] * 8,
        out_specs=anywhere,
        scratch_shapes=[
            pltpu.SMEM((BANDS, LANES), I32),
            pltpu.VMEM(FIELD, F32),
            pltpu.VMEM(FIELD, F32),
            dma, dma((PARTS,)),
        ] + [pltpu.VMEM((LF * 2 * NC, LANES), F32)] * COPIES,
        compiler_params=params(34),
        name="forcing_and_step",
    )(values, index, dense, held_x, held_y, below, side_in, rot)


def solution(mesh):
    placed = (
        P(None, "face", "rows", None),
        P(None, "face", "rows", None),
        P(None, "face", "rows", None),
        P("face", "rows", None, None),
        P("face", "rows", None),
        P("face", "rows", None),
        P("face", "rows", None),
    )
    return jax.shard_map(
        per_device,
        mesh=mesh,
        in_specs=placed,
        out_specs=P(None, "face", "rows", None),
        check_vma=False,
    )
```
